32 devices in a mesh: dp: 16 (over z, y, x), seq: 2 (over core).
Axes of the slice: x: 2, y: 2, z: 4, core: 2. Of those that a mesh axis runs over, the one named last changes fastest.
Arguments:
- patches: bfloat16 [64, 544, 768], P('dp', 'seq'), may hold values from -6 to 6
- lengths: int32 [64], P('dp'), may hold values from 40 to 529, as said below
- gain_one: float32 [768], replicated, may hold values from 0.5 to 1.5
- shift_one: float32 [768], replicated, may hold values from -2 to 2
- w_query: bfloat16 [768, 768], replicated, may hold values from -0.21875 to 0.21875
- b_query: float32 [768], replicated, may hold values from -2 to 2
- w_key: bfloat16 [768, 768], replicated, may hold values from -0.21875 to 0.21875
- w_value: bfloat16 [768, 768], replicated, may hold values from -0.21875 to 0.21875
- b_value: float32 [768], replicated, may hold values from -2 to 2
- w_out: bfloat16 [768, 768], replicated, may hold values from -1.75 to 1.75
- b_out: float32 [768], replicated, may hold values from -2 to 2
- gain_two: float32 [768], replicated, may hold values from 0.5 to 1.5
- shift_two: float32 [768], replicated, may hold values from -2 to 2
- w_up: bfloat16 [768, 3072], replicated, may hold values from -0.21875 to 0.21875
- b_up: float32 [3072], replicated, may hold values from -2 to 2
- w_down: bfloat16 [3072, 768], replicated, may hold values from -0.109375 to 0.109375
- b_down: float32 [768], replicated, may hold values from -2 to 2
- cotangent: bfloat16 [64, 544, 768], P('dp', 'seq'), may hold values from -6 to 6
Outputs:
- output: bfloat16 [64, 544, 768], P('dp', 'seq')
- grad_patches: bfloat16 [64, 544, 768], P('dp', 'seq')
- grad_gain_one: float32 [768], replicated
- grad_shift_one: float32 [768], replicated
- grad_w_query: float32 [768, 768], replicated
- grad_b_query: float32 [768], replicated
- grad_w_key: float32 [768, 768], replicated
- grad_w_value: float32 [768, 768], replicated
- grad_b_value: float32 [768], replicated
- grad_w_out: float32 [768, 768], replicated
- grad_b_out: float32 [768], replicated
- grad_gain_two: float32 [768], replicated
- grad_shift_two: float32 [768], replicated
- grad_w_up: float32 [768, 3072], replicated
- grad_b_up: float32 [3072], replicated
- grad_w_down: float32 [3072, 768], replicated
- grad_b_down: float32 [768], replicated
The draws below stay inside these ranges and needn't reach their ends.
Inputs may be any that keep to these rules, and one draw needn't show every extreme that they name: `lengths`: in each aligned block of 4 strips one strip has exactly 529 valid patches; valid patches come first in a strip.
All inputs are finite; a program needn't handle non-finite values.
Results may differ from the reference program's by a relative error of at most 0.012.
Values may be sent and summed in bfloat16 or wider, within the bound.
No kernel may reach another device: no remote copies, remote signals or barrier semaphores. Data moves between devices by JAX's collectives and lax.ppermute only.
A program may use at most 256 MiB of HBM per device.

```python
import jax
import jax.numpy as jnp
from jax import lax

D = 768
HEADS = 12
HEAD_DIM = 64
FF = 3072
SLOTS = 544
LMAX = 529
MIN_LEN = 40
STRIP_DEV = 4
STRIPS = 64


def draw_lengths(key, part):
    first_key, second_key = jax.random.split(key)
    base = jax.random.randint(first_key, (STRIPS,), MIN_LEN, LMAX + 1)
    picked = jax.random.randint(second_key, (STRIPS // STRIP_DEV,), 0, STRIP_DEV)
    position = jnp.arange(STRIPS, dtype=jnp.int32)
    in_block = position % STRIP_DEV
    block_index = position // STRIP_DEV
    chosen = picked[block_index]
    result = jnp.where(in_block == chosen, LMAX, base)
    result = jnp.where((block_index == 0) & (in_block == (chosen + 1) % STRIP_DEV), MIN_LEN, result)
    return result.astype(jnp.int32)


def levels(stream_key, extent, pieces, least, high):
    factor_of = 1.0
    for dim, parts in pieces:
        steps = jax.random.uniform(jax.random.fold_in(jax.random.fold_in(stream_key, 6), dim), (parts,), jnp.float32, least / len(pieces), high / len(pieces))
        factor_of = factor_of * jnp.repeat(jnp.exp(steps), extent[dim] // parts).reshape((-1,) + (1,) * (len(extent) - 1 - dim))
    return factor_of


def noise(rng, dims, width, bound, cuts=(), held_as=jnp.bfloat16):
    entries = width * jax.random.normal(rng, dims, jnp.float32)
    if cuts:
        entries = entries * levels(rng, dims, cuts, -0.22, 0.18)
    return jnp.clip(entries, -bound, bound).astype(held_as)


def setup_inputs(seed: int = 0) -> dict:
    streams_of = jax.random.split(jax.random.key(seed), 19)
    return {
        "patches": noise(streams_of[0], (STRIPS, SLOTS, D), 1.0, 6.0, ((0, 16), (1, 2))),
        "lengths": draw_lengths(jax.random.fold_in(streams_of[18], 71), 0),
        "gain_one": jnp.clip(1.0 + 0.1 * jax.random.normal(streams_of[2], (D,), jnp.float32), 0.5, 1.5),
        "shift_one": noise(streams_of[3], (D,), 0.3, 2.0, (), jnp.float32),
        "w_query": noise(streams_of[4], (D, D), D ** -0.5, 0.21875),
        "b_query": noise(streams_of[5], (D,), 0.3, 2.0, (), jnp.float32),
        "w_key": noise(streams_of[6], (D, D), D ** -0.5, 0.21875),
        "w_value": noise(streams_of[7], (D, D), D ** -0.5, 0.21875),
        "b_value": noise(streams_of[8], (D,), 0.3, 2.0, (), jnp.float32),
        "w_out": noise(streams_of[9], (D, D), (D // 64) ** -0.5, 1.75),
        "b_out": noise(streams_of[10], (D,), 0.3, 2.0, (), jnp.float32),
        "gain_two": jnp.clip(1.0 + 0.1 * jax.random.normal(streams_of[11], (D,), jnp.float32), 0.5, 1.5),
        "shift_two": noise(streams_of[12], (D,), 0.3, 2.0, (), jnp.float32),
        "w_up": noise(streams_of[13], (D, FF), D ** -0.5, 0.21875),
        "b_up": noise(streams_of[14], (FF,), 0.3, 2.0, (), jnp.float32),
        "w_down": noise(streams_of[15], (FF, D), FF ** -0.5, 0.109375),
        "b_down": noise(streams_of[16], (D,), 0.3, 2.0, (), jnp.float32),
        "cotangent": noise(streams_of[17], (STRIPS, SLOTS, D), 1.0, 6.0, ((0, 16), (1, 2))),
    }


epsilon = 1e-06

@jax.custom_vjp
def low(v):
    return lax.optimization_barrier(v.astype(jnp.bfloat16)).astype(jnp.float32)

@jax.custom_vjp
def low_back(v):
    return v

def low_keep(v):
    return (low(v), None)

def low_pass(kept, grad):
    return (grad,)

def back_keep(v):
    return (v, None)

def back_low(kept, grad):
    return (low(grad),)
low.defvjp(low_keep, low_pass)
low_back.defvjp(back_keep, back_low)

def product(left_rows, weight):
    return jnp.einsum('...d,df->...f', left_rows, weight, precision=lax.Precision.HIGHEST)

def layer_norm(values, gain, shift):
    centre = lax.optimization_barrier(jnp.mean(values, axis=-1, keepdims=True))
    centred = values - centre
    spread = lax.optimization_barrier(jnp.mean(centred * centred, axis=-1, keepdims=True))
    return centred * lax.rsqrt(spread + epsilon) * gain + shift

def forward(inputs, lengths, params):
    gain_one, shift_one, w_query, b_query, w_key, w_value, b_value, w_out, b_out, gain_two, shift_two, w_up, b_up, w_down, b_down = params
    groups = inputs.shape[0]
    normed = low(layer_norm(inputs, gain_one, shift_one))
    queries = low_back(low(product(normed, w_query) + b_query)).reshape(groups, SLOTS, HEADS, HEAD_DIM)
    key_rows = low_back(low(product(normed, w_key))).reshape(groups, SLOTS, HEADS, HEAD_DIM)
    value_rows = low_back(low(product(normed, w_value) + b_value)).reshape(groups, SLOTS, HEADS, HEAD_DIM)
    scores = jnp.einsum('gqhd,gkhd->ghqk', queries, key_rows, precision=lax.Precision.HIGHEST) * HEAD_DIM ** (-0.5)
    key_valid = jnp.arange(SLOTS, dtype=jnp.int32)[None, :] < lengths[:, None]
    scores = low_back(jnp.where(key_valid[:, None, None, :], scores, -jnp.inf))
    row_max = lax.optimization_barrier(jnp.max(scores, axis=-1, keepdims=True))
    exponent = jnp.exp(scores - row_max)
    attn_probs = low(exponent / lax.optimization_barrier(jnp.sum(exponent, axis=-1, keepdims=True)))
    context = jnp.einsum('ghqk,gkhd->gqhd', attn_probs, value_rows, precision=lax.Precision.HIGHEST)
    context = low_back(low(context.reshape(groups, SLOTS, HEADS * HEAD_DIM)))
    hidden = inputs + low_back(product(context, w_out) + b_out)
    normed_two = low(layer_norm(hidden, gain_two, shift_two))
    upper_pre = low_back(product(normed_two, w_up) + b_up)
    active = low(jax.nn.gelu(upper_pre, approximate=False))
    return hidden + low_back(product(active, w_down) + b_down)

def reference(patches, lengths, gain_one, shift_one, w_query, b_query, w_key, w_value, b_value, w_out, b_out, gain_two, shift_two, w_up, b_up, w_down, b_down, cotangent):
    params = tuple((p.astype(jnp.float32) for p in (gain_one, shift_one, w_query, b_query, w_key, w_value, b_value, w_out, b_out, gain_two, shift_two, w_up, b_up, w_down, b_down)))
    blocks = STRIPS // STRIP_DEV
    inputs = patches.astype(jnp.float32).reshape(blocks, STRIP_DEV, SLOTS, D)
    grads_in = cotangent.astype(jnp.float32).reshape(blocks, STRIP_DEV, SLOTS, D)
    length_blocks = lengths.reshape(blocks, STRIP_DEV)

    def step(totals, block_item):
        block_inputs, block_lengths, block_cotangent = block_item

        def apply(block_x, block_params):
            return forward(block_x, block_lengths, block_params)
        result, pullback = jax.vjp(apply, block_inputs, params)
        grad_inputs, grad_params = pullback(block_cotangent)
        totals = jax.tree.map(jnp.add, totals, grad_params)
        return (totals, (result.astype(jnp.bfloat16), grad_inputs.astype(jnp.bfloat16)))
    start = jax.tree.map(jnp.zeros_like, params)
    totals, (results, grad_inputs) = lax.scan(step, start, (inputs, length_blocks, grads_in))
    return (results.reshape(STRIPS, SLOTS, D), grad_inputs.reshape(STRIPS, SLOTS, D), totals[0], totals[1], totals[2], totals[3], totals[4], totals[5], totals[6], totals[7], totals[8], totals[9], totals[10], totals[11], totals[12], totals[13], totals[14])
```

```python
import functools

import jax
import jax.numpy as jnp
from jax import lax
from jax.experimental import pallas as pl
from jax.experimental.pallas import tpu as pltpu
from jax.sharding import PartitionSpec as P

F32, BF16 = jnp.float32, jnp.bfloat16
D, HEADS, HEAD_DIM, FF, SLOTS = 768, 12, 64, 3072, 544
STRIPS = 2
ROWS = STRIPS * SLOTS
PAIRS = HEADS // 2
EPS = 1e-06
MASKED = -1e30
GROUPS = 3
GROUP_PAIRS = PAIRS // GROUPS
GCOLS = D // GROUPS
MLP_CALLS = 2
MLP_STEPS = 4
FSTEP = FF // (MLP_CALLS * MLP_STEPS)
FCALL = FF // MLP_CALLS
VMEM = 58 * 1024 * 1024


def params(vmem=VMEM, grid=1):
    return pltpu.CompilerParams(
        vmem_limit_bytes=vmem, dimension_semantics=("arbitrary",) * grid
    )


def dot(a, b):
    return lax.dot_general(a, b, (((1,), (0,)), ((), ())), preferred_element_type=F32)


def dot_bt(a, b):
    return lax.dot_general(a, b, (((1,), (1,)), ((), ())), preferred_element_type=F32)


def dot_at(a, b):
    return lax.dot_general(a, b, (((0,), (0,)), ((), ())), preferred_element_type=F32)


def norm_parts(values):
    centre = jnp.mean(values, axis=-1, keepdims=True)
    centred = values - centre
    spread = jnp.mean(centred * centred, axis=-1, keepdims=True)
    rstd = lax.rsqrt(spread + EPS)
    return centred * rstd, rstd


def gelu_parts(u):
    t = 1.0 / (1.0 + (0.3275911 * 0.7071067811865476) * jnp.abs(u))
    e = jnp.exp(-0.5 * u * u)
    poly = 0.5 * 1.061405429 * t + 0.5 * -1.453152027
    poly = poly * t + 0.5 * 1.421413741
    poly = poly * t + 0.5 * -0.284496736
    poly = poly * t + 0.5 * 0.254829592
    tail = poly * t * e
    cdf = jnp.where(u >= 0, 1.0 - tail, tail)
    return u * cdf, cdf + u * (e * 0.3989422804014327)


def split3(x):
    hi = x.astype(BF16).astype(F32)
    rest = x - hi
    mid = rest.astype(BF16).astype(F32)
    return hi, mid, rest - mid


def lane_iota():
    return lax.broadcasted_iota(jnp.int32, (SLOTS, 128), 1)


def half_mask(lane, h):
    return jnp.where((lane >= 64 * h) & (lane < 64 * h + 64), 1.0, 0.0).astype(BF16)


def key_extra(lane, length, h):
    first = 64 * (1 - h)
    row = lax.broadcasted_iota(jnp.int32, (SLOTS, 128), 0)
    bias = jnp.where(row < length, 0.0, MASKED)
    ones = (lane > first) & (lane < first + 4)
    return jnp.where(lane == first, bias, jnp.where(ones, 1.0, 0.0)).astype(BF16)


def pieces_extra(lane, column, h, lead):
    first = 64 * (1 - h)
    hi, mid, low = split3(column)
    out = jnp.where(lane == first + 3, low, jnp.where(lane == first, lead, 0.0))
    out = jnp.where(lane == first + 2, mid, out)
    return jnp.where(lane == first + 1, hi, out).astype(BF16)


def attend_kernel(
    len_ref, x_ref, g1_ref, s1_ref, wq_ref, bq_ref, wk_ref, wv_ref, bv_ref, wo_ref, bo_ref, g2_ref, s2_ref,
    n1_ref, qa_ref, k_ref, v_ref, ctx_ref, hid_ref, n2_ref, q_scr,
):
    x = x_ref[0].astype(F32)
    scaled, _ = norm_parts(x)
    n1 = (scaled * g1_ref[...] + s1_ref[...]).astype(BF16)
    n1_ref[0] = n1
    q_scr[...] = ((dot(n1, wq_ref[...]) + bq_ref[...]).astype(BF16).astype(F32) * (HEAD_DIM**-0.5)).astype(BF16)
    k_ref[0] = dot(n1, wk_ref[...]).astype(BF16)
    v_ref[0] = (dot(n1, wv_ref[...]) + bv_ref[...]).astype(BF16)
    length = len_ref[pl.program_id(0)]
    lane = lane_iota()
    own = [half_mask(lane, h) for h in (0, 1)]
    kx = [key_extra(lane, length, h) for h in (0, 1)]

    def pair(p, _):
        cols = pl.ds(pl.multiple_of(p * 128, 128), 128)
        qp, kp, vp = q_scr[:, cols], k_ref[0, :, cols], v_ref[0, :, cols]
        ctx = None
        inverses = []
        for h in (0, 1):
            first = 64 * (1 - h)
            query = qp * own[h] + jnp.where(lane == first, 1.0, 0.0).astype(BF16)
            scores = dot_bt(query, kp * own[h] + kx[h])
            top = jnp.max(scores, axis=-1, keepdims=True)
            weights = jnp.exp(scores - top)
            total = jnp.sum(weights, axis=-1, keepdims=True)
            part = dot(weights.astype(BF16), vp * own[h])
            ctx = part if ctx is None else ctx + part
            inverses.append(1.0 / total)
            extra = pieces_extra(lane, -(top + jnp.log(total)), h, 1.0)
            qa_ref[0, :, pl.ds(pl.multiple_of(p * 256 + 128 * h, 128), 128)] = qp * own[h] + extra
        scale = jnp.where(lane < 64, inverses[0], inverses[1])
        ctx_ref[0, :, cols] = (ctx * scale).astype(BF16)
        return 0

    lax.fori_loop(0, PAIRS, pair, 0)
    hidden = x + dot(ctx_ref[0], wo_ref[...]) + bo_ref[...]
    hid_ref[0] = hidden
    scaled, _ = norm_parts(hidden)
    n2_ref[0] = (scaled * g2_ref[...] + s2_ref[...]).astype(BF16)


def whole(shape):
    return pl.BlockSpec(shape, lambda *_: (0,) * len(shape))


def strip_block(cols):
    return pl.BlockSpec((1, SLOTS, cols), lambda s, *_: (s, 0, 0))


def strips_of(cols, dtype):
    return jax.ShapeDtypeStruct((STRIPS, SLOTS, cols), dtype)


def attend(lens, x, g1, s1, wq, bq, wk, wv, bv, wo, bo, g2, s2):
    vec, mat = whole((1, D)), whole((D, D))
    return pl.pallas_call(
        attend_kernel,
        grid_spec=pltpu.PrefetchScalarGridSpec(
            num_scalar_prefetch=1,
            grid=(STRIPS,),
            in_specs=[strip_block(D), vec, vec, mat, vec, mat, mat, vec, mat, vec, vec, vec],
            out_specs=[strip_block(D), strip_block(2 * D)] + [strip_block(D)] * 5,
            scratch_shapes=[pltpu.VMEM((SLOTS, D), BF16)],
        ),
        out_shape=[strips_of(D, BF16), strips_of(2 * D, BF16), strips_of(D, BF16), strips_of(D, BF16),
                   strips_of(D, BF16), strips_of(D, F32), strips_of(D, BF16)],
        compiler_params=params(),
        name="attend",
    )(lens, x, g1, s1, wq, bq, wk, wv, bv, wo, bo, g2, s2)


def mlp_kernel(
    first, last, at_ref, n2_ref, cot_ref, up_ref, bup_ref, dn_ref, bdn_ref, acc_in_ref, *rest
):
    if first:
        gn_in_ref = None
    else:
        gn_in_ref, rest = rest[0], rest[1:]
    keep_ref, send_ref, out_ref, gn_ref, gbup_ref, a_scr, g_scr = rest[:7]
    acc_ref = rest[7] if last else out_ref
    step = pl.program_id(0)

    @pl.when(step == 0)
    def _():
        acc_ref[...] = acc_in_ref[...] + bdn_ref[...] if first else acc_in_ref[...]
        gn_ref[...] = jnp.zeros_like(gn_ref) if first else gn_in_ref[...]

    up, down, bias = up_ref[...], dn_ref[...], bup_ref[...]
    sums = None
    for r in range(0, ROWS, SLOTS):
        rows = slice(r, r + SLOTS)
        u = dot(n2_ref[rows], up) + bias
        grad_active = dot_bt(cot_ref[rows], down)
        active, slope = gelu_parts(u)
        active = active.astype(BF16)
        grad_upper = (grad_active * slope).astype(BF16)
        a_scr[rows] = active
        g_scr[rows] = grad_upper
        acc_ref[rows] += dot(active, down)
        gn_ref[rows] += dot_bt(grad_upper, up)
        part = jnp.sum(grad_upper.astype(F32), axis=0, keepdims=True)
        sums = part if sums is None else sums + part
    gbup_ref[...] = sums
    grad_down = dot_at(a_scr[...], cot_ref[...]).astype(BF16)
    grad_up = dot_at(n2_ref[...], g_scr[...]).astype(BF16)
    core, place = at_ref[0], at_ref[1]
    chunk = FCALL // 16
    per_step = FSTEP // chunk
    rows_up = D // 16
    half, col = step // 2, lax.rem(step, 2)

    def put(down_ref, up_out_ref):
        for i in range(per_step):
            down_ref[(step * per_step + i) ^ place] = grad_down[i * chunk : (i + 1) * chunk]
        for i in range(16):
            up_out_ref[
                i ^ place,
                pl.ds(pl.multiple_of(half * rows_up, 16), rows_up),
                pl.ds(pl.multiple_of(col * FSTEP, 128), FSTEP),
            ] = grad_up[i * rows_up : (i + 1) * rows_up]

    @pl.when(core == 0)
    def _():
        put(keep_ref, send_ref)

    @pl.when(core == 1)
    def _():
        put(send_ref, keep_ref)

    if last:
        @pl.when(step == MLP_STEPS - 1)
        def _():
            out_ref[...] = acc_ref[...].astype(BF16)


def mlp(call, at, n2, cot, w_up, b_up, w_down, b_down, acc, gn):
    first, last = call == 0, call == MLP_CALLS - 1
    base = call * MLP_STEPS
    piece = jax.ShapeDtypeStruct((16, FCALL // 16, D), BF16)
    rows = whole((ROWS, D))
    in_specs = [
        rows, rows,
        pl.BlockSpec((D, FSTEP), lambda s, *_: (0, base + s)),
        pl.BlockSpec((1, FSTEP), lambda s, *_: (0, base + s)),
        pl.BlockSpec((FSTEP, D), lambda s, *_: (base + s, 0)),
        whole((1, D)), rows,
    ]
    operands = [n2, cot, w_up, b_up, w_down, b_down, acc]
    if not first:
        in_specs.append(rows)
        operands.append(gn)
    return pl.pallas_call(
        functools.partial(mlp_kernel, first, last),
        grid_spec=pltpu.PrefetchScalarGridSpec(
            num_scalar_prefetch=1,
            grid=(MLP_STEPS,),
            in_specs=in_specs,
            out_specs=[whole(piece.shape), whole(piece.shape), rows, rows,
                       pl.BlockSpec((1, FSTEP), lambda s, *_: (0, s))],
            scratch_shapes=[pltpu.VMEM((ROWS, FSTEP), BF16)] * 2
            + ([pltpu.VMEM((ROWS, D), F32)] if last else []),
        ),
        out_shape=[piece, piece, jax.ShapeDtypeStruct((ROWS, D), BF16 if last else F32),
                   jax.ShapeDtypeStruct((ROWS, D), F32), jax.ShapeDtypeStruct((1, FCALL), F32)],
        compiler_params=params(),
        name="mlp",
    )(at, *operands)


def mid_kernel(
    at_ref, gn_ref, hid_ref, cot_ref, ctx_ref, wo_ref, g2_ref,
    gh_ref, dctx_ref, gwo_ref, ggain_ref, gshift_ref, gbo_ref, gbdn_ref, acc_scr,
):
    strip = pl.program_id(0)
    grad = gn_ref[0]
    cot = cot_ref[0].astype(F32)
    scaled, rstd = norm_parts(hid_ref[0])
    t = grad * g2_ref[...]
    cross = jnp.mean(t * scaled, axis=-1, keepdims=True)
    grad_hidden = cot + rstd * (t - jnp.mean(t, axis=-1, keepdims=True) - scaled * cross)
    gh_ref[0] = grad_hidden
    grad_attn = grad_hidden.astype(BF16)
    dctx_ref[0] = dot_bt(grad_attn, wo_ref[...]).astype(BF16)
    grad_out = dot_at(ctx_ref[0], grad_attn)
    sums = [
        jnp.sum(grad * scaled, axis=0, keepdims=True),
        jnp.sum(grad, axis=0, keepdims=True),
        jnp.sum(grad_attn.astype(F32), axis=0, keepdims=True),
        jnp.sum(cot, axis=0, keepdims=True),
    ]
    refs = [ggain_ref, gshift_ref, gbo_ref, gbdn_ref]

    @pl.when(strip == 0)
    def _():
        acc_scr[...] = grad_out
        for ref, value in zip(refs, sums):
            ref[...] = value

    @pl.when(strip > 0)
    def _():
        total = (acc_scr[...] + grad_out).astype(BF16)
        for i in range(16):
            gwo_ref[i ^ at_ref[1]] = total[i * 48 : (i + 1) * 48]
        for ref, value in zip(refs, sums):
            ref[...] += value


def middle(at, gn, hid, cot, ctx, wo, g2):
    vec = jax.ShapeDtypeStruct((1, D), F32)
    return pl.pallas_call(
        mid_kernel,
        grid_spec=pltpu.PrefetchScalarGridSpec(
            num_scalar_prefetch=1,
            grid=(STRIPS,),
            in_specs=[strip_block(D)] * 4 + [whole((D, D)), whole((1, D))],
            out_specs=[strip_block(D), strip_block(D), whole((16, 48, D))] + [whole((1, D))] * 4,
            scratch_shapes=[pltpu.VMEM((D, D), F32)],
        ),
        out_shape=[strips_of(D, F32), strips_of(D, BF16), jax.ShapeDtypeStruct((16, 48, D), BF16)] + [vec] * 4,
        compiler_params=params(),
        name="middle",
    )(at, gn, hid, cot, ctx, wo, g2)


def back_kernel(
    first, at_ref, len_ref, qa_ref, k_ref, v_ref, dctx_ref, ctx_ref, n1_ref, wq_ref, wk_ref, wv_ref, *rest
):
    if first:
        gn_in_ref = None
    else:
        gn_in_ref, rest = rest[0], rest[1:]
    grads_ref, gn_ref, sums_ref, d_scr, acc_scr = rest
    strip = pl.program_id(0)
    lane = lane_iota()
    own = [half_mask(lane, h) for h in (0, 1)]
    length = len_ref[strip]
    kx = [key_extra(lane, length, h) for h in (0, 1)]
    vx = [
        jnp.where((lane > 64 * (1 - h)) & (lane < 64 * (1 - h) + 4), 1.0, 0.0).astype(BF16)
        for h in (0, 1)
    ]
    for p in range(GROUP_PAIRS):
        cols = slice(p * 128, p * 128 + 128)
        kp, vp, dp, cp = k_ref[0, :, cols], v_ref[0, :, cols], dctx_ref[0, :, cols], ctx_ref[0, :, cols]
        product = dp.astype(F32) * cp.astype(F32)
        dq, dk, dv = [], [], []
        for h in (0, 1):
            query = qa_ref[0, :, p * 256 + 128 * h : p * 256 + 128 * h + 128]
            inner = jnp.sum(product * own[h].astype(F32), axis=-1, keepdims=True)
            grad = dp * own[h] + pieces_extra(lane, -inner, h, 0.0)
            probs = jnp.exp(dot_bt(kp * own[h] + kx[h], query))
            grad_scores = (probs * dot_bt(vp * own[h] + vx[h], grad)).astype(BF16)
            dv.append(dot(probs.astype(BF16), dp))
            dk.append(dot(grad_scores, query))
            dq.append(dot_at(grad_scores, kp))
        low = lane < 64
        d_scr[:, cols] = (jnp.where(low, dq[0], dq[1]) * (HEAD_DIM**-0.5)).astype(BF16)
        d_scr[:, GCOLS + p * 128 : GCOLS + p * 128 + 128] = jnp.where(low, dk[0], dk[1]).astype(BF16)
        d_scr[:, 2 * GCOLS + p * 128 : 2 * GCOLS + p * 128 + 128] = jnp.where(low, dv[0], dv[1]).astype(BF16)
    d_all = d_scr[...]
    back = dot_bt(d_all[:, :GCOLS], wq_ref[...])
    back += dot_bt(d_all[:, GCOLS : 2 * GCOLS], wk_ref[...])
    back += dot_bt(d_all[:, 2 * GCOLS :], wv_ref[...])
    gn_ref[0] = back if first else back + gn_in_ref[0]
    grad = dot_at(n1_ref[0], d_all)
    sums = jnp.sum(d_all.astype(F32), axis=0, keepdims=True)

    @pl.when(strip == 0)
    def _():
        acc_scr[...] = grad
        sums_ref[...] = sums

    @pl.when(strip > 0)
    def _():
        total = (acc_scr[...] + grad).astype(BF16)
        for i in range(16):
            grads_ref[i ^ at_ref[1]] = total[i * 48 : (i + 1) * 48]
        sums_ref[...] += sums


def attend_back(group, at, lens, qa, k, v, dctx, ctx, n1, wq, wk, wv, gn):
    first = group == 0

    def cols(width):
        return pl.BlockSpec((1, SLOTS, width), lambda s, *_: (s, 0, group))

    weight = pl.BlockSpec((D, GCOLS), lambda s, *_: (0, group))
    in_specs = [cols(2 * GCOLS)] + [cols(GCOLS)] * 4 + [strip_block(D)] + [weight] * 3
    operands = [qa, k, v, dctx, ctx, n1, wq, wk, wv]
    if not first:
        in_specs.append(strip_block(D))
        operands.append(gn)
    return pl.pallas_call(
        functools.partial(back_kernel, first),
        grid_spec=pltpu.PrefetchScalarGridSpec(
            num_scalar_prefetch=2,
            grid=(STRIPS,),
            in_specs=in_specs,
            out_specs=[whole((16, 48, D)), strip_block(D), whole((1, 3 * GCOLS))],
            scratch_shapes=[pltpu.VMEM((SLOTS, 3 * GCOLS), BF16), pltpu.VMEM((D, 3 * GCOLS), F32)],
        ),
        out_shape=[jax.ShapeDtypeStruct((16, 48, D), BF16), strips_of(D, F32),
                   jax.ShapeDtypeStruct((1, 3 * GCOLS), F32)],
        compiler_params=params(),
        name="attend_back",
    )(at, lens, *operands)


def end_kernel(gn_ref, x_ref, gh_ref, g1_ref, gp_ref, ggain_ref, gshift_ref):
    strip = pl.program_id(0)
    grad = gn_ref[0]
    scaled, rstd = norm_parts(x_ref[0].astype(F32))
    t = grad * g1_ref[...]
    cross = jnp.mean(t * scaled, axis=-1, keepdims=True)
    grad_in = rstd * (t - jnp.mean(t, axis=-1, keepdims=True) - scaled * cross)
    gp_ref[0] = (gh_ref[0] + grad_in).astype(BF16)
    sums = [jnp.sum(grad * scaled, axis=0, keepdims=True), jnp.sum(grad, axis=0, keepdims=True)]

    @pl.when(strip == 0)
    def _():
        ggain_ref[...], gshift_ref[...] = sums

    @pl.when(strip > 0)
    def _():
        ggain_ref[...] += sums[0]
        gshift_ref[...] += sums[1]


def end(gn, x, gh, g1):
    vec = jax.ShapeDtypeStruct((1, D), F32)
    return pl.pallas_call(
        end_kernel,
        grid=(STRIPS,),
        in_specs=[strip_block(D)] * 3 + [whole((1, D))],
        out_specs=[strip_block(D)] + [whole((1, D))] * 2,
        out_shape=[strips_of(D, BF16), vec, vec],
        compiler_params=params(),
        name="end",
    )(gn, x, gh, g1)


def widen_mlp_kernel(at_ref, mine_ref, other_ref, *rest):
    down_ref, up_ref = rest[-2:]
    swap = at_ref[0] == 1
    mine, other = mine_ref[0], other_ref[0]
    down_ref[...] = jnp.where(swap, other, mine).astype(F32)
    up = jnp.where(swap, mine, other).astype(F32)
    up_ref[:, :D] = up[:48]
    up_ref[:, D:] = up[48:]


def widen_mlp(call, at, mine, other, given):
    block = pl.BlockSpec((1, FCALL // 16, D), lambda i, at_ref: (i ^ at_ref[1], 0, 0))
    operands = [mine, other] + list(given)
    return pl.pallas_call(
        widen_mlp_kernel,
        grid_spec=pltpu.PrefetchScalarGridSpec(
            num_scalar_prefetch=1,
            grid=(16,),
            in_specs=[block, block] + [pl.BlockSpec(memory_space=pl.ANY)] * len(given),
            out_specs=[
                pl.BlockSpec((FCALL // 16, D), lambda i, *_: (16 * call + i, 0)),
                pl.BlockSpec((D // 16, FCALL), lambda i, *_: (i, call)),
            ],
        ),
        out_shape=[jax.ShapeDtypeStruct((FF, D), F32), jax.ShapeDtypeStruct((D, FF), F32)],
        input_output_aliases={3: 0, 4: 1} if given else {},
        compiler_params=params(),
        name="widen_mlp",
    )(at, *operands)


def widen_attn_kernel(at_ref, mine_ref, other_ref, out_ref, q_ref, k_ref, v_ref):
    swap = at_ref[0] == 1
    mine, other = mine_ref[0], other_ref[0]
    low = jnp.where(swap, other, mine).astype(F32)
    high = jnp.where(swap, mine, other).astype(F32)
    out_ref[...] = low[:48]
    for g, block in enumerate((low[48:], high[:48], high[48:])):
        cols = slice(g * GCOLS, (g + 1) * GCOLS)
        q_ref[:, cols] = block[:, :GCOLS]
        k_ref[:, cols] = block[:, GCOLS : 2 * GCOLS]
        v_ref[:, cols] = block[:, 2 * GCOLS :]


def widen_attn(at, mine, other):
    block = pl.BlockSpec((1, 96, D), lambda i, at_ref: (i ^ at_ref[1], 0, 0))
    return pl.pallas_call(
        widen_attn_kernel,
        grid_spec=pltpu.PrefetchScalarGridSpec(
            num_scalar_prefetch=1,
            grid=(16,),
            in_specs=[block, block],
            out_specs=[pl.BlockSpec((48, D), lambda i, *_: (i, 0))] * 4,
        ),
        out_shape=[jax.ShapeDtypeStruct((D, D), F32)] * 4,
        compiler_params=params(),
        name="widen_attn",
    )(at, mine, other)


def swap(value, axis, bit, size):
    return lax.ppermute(value, axis, [(i, i ^ bit) for i in range(size)])


def sum_scatter(keep, send, bits, dp):
    total = keep + swap(send, "seq", 1, 2)
    for step, bit in enumerate(bits):
        if step < 4:
            half = total.shape[0] // 2
            total = total[:half] + swap(total[half:], "dp", bit, dp)
        else:
            total = total + swap(total, "dp", bit, dp)
    return total


def gather(total, bits, dp):
    for bit in reversed(bits[:4]):
        total = jnp.concatenate([total, swap(total, "dp", bit, dp)], axis=0)
    return total, swap(total, "seq", 1, 2)


def local(
    dp, patches, lengths, gain_one, shift_one, w_query, b_query, w_key, w_value, b_value, w_out, b_out,
    gain_two, shift_two, w_up, b_up, w_down, b_down, cotangent,
):
    core, block = lax.axis_index("seq"), lax.axis_index("dp")
    bits = [1 << i for i in range(dp.bit_length() - 1)]

    def order_of(bits):
        place = jnp.int32(0)
        for bit in bits[:4]:
            place = place * 2 + jnp.where((block & bit) != 0, 1, 0)
        return jnp.stack([core, place]).astype(jnp.int32)

    row = lambda v: v.reshape(1, -1)
    strips = lambda v: lax.all_to_all(v, "seq", split_axis=0, concat_axis=1, tiled=True)
    slots = lambda v: lax.all_to_all(v, "seq", split_axis=1, concat_axis=0, tiled=True)
    x, cot = strips(patches), strips(cotangent)
    lens = lax.dynamic_slice(lengths, (core * STRIPS,), (STRIPS,))
    n1, qa, k, v, ctx, hid, n2 = attend(
        lens, x, row(gain_one), row(shift_one), w_query, row(b_query), w_key, w_value, row(b_value),
        w_out, row(b_out), row(gain_two), row(shift_two),
    )
    flat = lambda v: v.reshape(ROWS, D)
    acc, gn = flat(hid), None
    at = order_of(bits)
    pieces, g_bup = [], []
    for call in range(MLP_CALLS):
        keep, send, acc, gn, sums = mlp(
            call, at, flat(n2), flat(cot), w_up, row(b_up), w_down, row(b_down), acc, gn
        )
        pieces.append((keep, send))
        g_bup.append(sums)
    output = slots(acc.reshape(STRIPS, SLOTS, D))
    gh, dctx, g_out, g_gain_two, g_shift_two, g_bout, g_bdown = middle(
        at, gn.reshape(STRIPS, SLOTS, D), hid, cot, ctx, w_out, row(gain_two)
    )
    gn, blocks, sums = None, [g_out], []
    for group in range(GROUPS):
        grads, gn, part = attend_back(
            group, at, lens, qa, k, v, dctx, ctx, n1, w_query, w_key, w_value, gn
        )
        blocks.append(grads)
        sums.append(part)
    gp, g_gain_one, g_shift_one = end(gn, x, gh, row(gain_one))
    grad_patches = slots(gp)
    low = jnp.concatenate(blocks[:2], axis=1)
    high = jnp.concatenate(blocks[2:], axis=1)
    pieces.append((jnp.where(core == 0, low, high), jnp.where(core == 0, high, low)))
    g_bquery = jnp.concatenate([s[:, :GCOLS] for s in sums], axis=1)
    g_bvalue = jnp.concatenate([s[:, 2 * GCOLS :] for s in sums], axis=1)
    small = [g_gain_one, g_shift_one, g_bquery, g_bvalue, g_bout, g_gain_two, g_shift_two, g_bdown] + g_bup
    small = lax.psum(jnp.concatenate(small, axis=1), ("dp", "seq"))[0]
    vecs = [small[i * D : (i + 1) * D] for i in range(8)]
    g_bup = small[8 * D :]
    given = ()
    for call in range(MLP_CALLS):
        mine, other = gather(sum_scatter(*pieces[call], bits, dp), bits, dp)
        given = widen_mlp(call, at, mine, other, given)
    g_down, g_up = given
    mine, other = gather(sum_scatter(*pieces[-1], bits, dp), bits, dp)
    g_out, g_query, g_key, g_value = widen_attn(at, mine, other)
    return (
        output, grad_patches, vecs[0], vecs[1], g_query, vecs[2], g_key, g_value, vecs[3], g_out, vecs[4],
        vecs[5], vecs[6], g_up, g_bup, g_down, vecs[7],
    )


def solution(mesh):
    dp = mesh.shape["dp"]
    rows, rep = P("dp", "seq", None), P()
    return jax.shard_map(
        functools.partial(local, dp),
        mesh=mesh,
        in_specs=(rows, P("dp")) + (rep,) * 15 + (rows,),
        out_specs=(rows, rows) + (rep,) * 15,
        check_vma=False,
    )
```

```python
import functools

import jax
import jax.numpy as jnp
from jax import lax
from jax.experimental import pallas as pl
from jax.experimental.pallas import tpu as pltpu
from jax.sharding import PartitionSpec as P

F32, BF16 = jnp.float32, jnp.bfloat16
D, HEADS, HEAD_DIM, FF, SLOTS = 768, 12, 64, 3072, 544
X_LAST, Y_LAST = (8, 4, 2, 1), (8, 4, 1, 2)
STRIPS = 2
ROWS = STRIPS * SLOTS
PAIRS = HEADS // 2
EPS = 1e-06
MASKED = -1e30
GROUPS = 3
GROUP_PAIRS = PAIRS // GROUPS
GCOLS = D // GROUPS
HALF = SLOTS // 2
FSTEP = 768
PIECE_STEPS = 2
FCALL = FSTEP * PIECE_STEPS
GAIN_1, SHIFT_1, B_QUERY, B_VALUE, B_OUT, GAIN_2, SHIFT_2, B_DOWN, B_UP = range(9)
VECTORS = B_UP + FF // D
SMALL = 16


def params(mib):
    return pltpu.CompilerParams(vmem_limit_bytes=mib << 20, dimension_semantics=("arbitrary",))


def far(value):
    return pltpu.with_memory_space_constraint(value, pltpu.HBM)


def cost(micros):
    return pl.CostEstimate(flops=int(micros * 1.15e10), bytes_accessed=0, transcendentals=0)


def call(kernel, operands, in_specs, after, prefetch=0, micros=10, mib=16, **kw):
    after = [v for v in after if v is not None]
    count = len(after)
    scalars = operands[:prefetch]

    def body(*refs):
        n = prefetch + len(in_specs)
        kernel(*refs[:n], *refs[n + count :])

    spec = pltpu.PrefetchScalarGridSpec(
        num_scalar_prefetch=prefetch,
        grid=kw.pop("grid"),
        in_specs=list(in_specs) + [pl.BlockSpec(memory_space=pl.ANY)] * count,
        out_specs=kw.pop("out_specs"),
        scratch_shapes=kw.pop("scratch_shapes", []),
    )
    return pl.pallas_call(body, grid_spec=spec, compiler_params=params(mib), cost_estimate=cost(micros), **kw)(
        *operands, *after
    )


def dot(a, b):
    return lax.dot_general(a, b, (((1,), (0,)), ((), ())), preferred_element_type=F32)


def dot_bt(a, b):
    return lax.dot_general(a, b, (((1,), (1,)), ((), ())), preferred_element_type=F32)


def dot_at(a, b):
    return lax.dot_general(a, b, (((0,), (0,)), ((), ())), preferred_element_type=F32)


def norm_parts(values):
    centre = jnp.mean(values, axis=-1, keepdims=True)
    centred = values - centre
    spread = jnp.mean(centred * centred, axis=-1, keepdims=True)
    rstd = lax.rsqrt(spread + EPS)
    return centred * rstd, rstd


def gelu_parts(u):
    t = 1.0 / (1.0 + (0.3275911 * 0.7071067811865476) * jnp.abs(u))
    e = jnp.exp(-0.5 * u * u)
    poly = 0.5 * 1.061405429 * t + 0.5 * -1.453152027
    poly = poly * t + 0.5 * 1.421413741
    poly = poly * t + 0.5 * -0.284496736
    poly = poly * t + 0.5 * 0.254829592
    tail = poly * t * e
    cdf = jnp.where(u >= 0, 1.0 - tail, tail)
    return u * cdf, cdf + u * (e * 0.3989422804014327)


def split3(x):
    hi = x.astype(BF16).astype(F32)
    rest = x - hi
    mid = rest.astype(BF16).astype(F32)
    return hi, mid, rest - mid


def lane_iota():
    return lax.broadcasted_iota(jnp.int32, (SLOTS, 128), 1)


def half_mask(lane, h):
    return jnp.where((lane >= 64 * h) & (lane < 64 * h + 64), 1.0, 0.0).astype(BF16)


def key_extra(lane, length, h):
    first = 64 * (1 - h)
    row = lax.broadcasted_iota(jnp.int32, (SLOTS, 128), 0)
    bias = jnp.where(row < length, 0.0, MASKED)
    ones = (lane > first) & (lane < first + 4)
    return jnp.where(lane == first, bias, jnp.where(ones, 1.0, 0.0)).astype(BF16)


def pieces_extra(lane, column, h, lead):
    first = 64 * (1 - h)
    hi, mid, low = split3(column)
    out = jnp.where(lane == first + 3, low, jnp.where(lane == first, lead, 0.0))
    out = jnp.where(lane == first + 2, mid, out)
    return jnp.where(lane == first + 1, hi, out).astype(BF16)


def row_of(ref, i):
    return ref[i : i + 1]


def attend_kernel(
    at_ref, len_ref, own_ref, got_ref, own_cot_ref, got_cot_ref, vec_ref, wq_ref, wk_ref, wv_ref, wo_ref,
    n1_ref, qa_ref, k_ref, v_ref, ctx_ref, hid_ref, n2_ref, x_ref, cot_ref, q_scr,
):
    core = at_ref[0]
    own_rows = pl.ds(pl.multiple_of(core * HALF, 16), HALF)
    got_rows = pl.ds(pl.multiple_of((1 - core) * HALF, 16), HALF)
    x_ref[0, own_rows], x_ref[0, got_rows] = own_ref[0], got_ref[0]
    cot_ref[0, own_rows], cot_ref[0, got_rows] = own_cot_ref[0], got_cot_ref[0]
    x = x_ref[0].astype(F32)
    scaled, _ = norm_parts(x)
    n1 = (scaled * row_of(vec_ref, GAIN_1) + row_of(vec_ref, SHIFT_1)).astype(BF16)
    n1_ref[0] = n1
    queries = (dot(n1, wq_ref[...]) + row_of(vec_ref, B_QUERY)).astype(BF16)
    q_scr[...] = (queries.astype(F32) * (HEAD_DIM**-0.5)).astype(BF16)
    k_ref[0] = dot(n1, wk_ref[...]).astype(BF16)
    v_ref[0] = (dot(n1, wv_ref[...]) + row_of(vec_ref, B_VALUE)).astype(BF16)
    length = len_ref[STRIPS * core + pl.program_id(0)]
    lane = lane_iota()
    own = [half_mask(lane, h) for h in (0, 1)]
    kx = [key_extra(lane, length, h) for h in (0, 1)]

    def pair(p, _):
        cols = pl.ds(pl.multiple_of(p * 128, 128), 128)
        qp, kp, vp = q_scr[:, cols], k_ref[0, :, cols], v_ref[0, :, cols]
        ctx = None
        inverses = []
        for h in (0, 1):
            first = 64 * (1 - h)
            query = qp * own[h] + jnp.where(lane == first, 1.0, 0.0).astype(BF16)
            scores = dot_bt(query, kp * own[h] + kx[h])
            top = jnp.max(scores, axis=-1, keepdims=True)
            weights = jnp.exp(scores - top)
            total = jnp.sum(weights, axis=-1, keepdims=True)
            part = dot(weights.astype(BF16), vp * own[h])
            ctx = part if ctx is None else ctx + part
            inverses.append(1.0 / total)
            extra = pieces_extra(lane, -(top + jnp.log(total)), h, 1.0)
            qa_ref[0, :, pl.ds(pl.multiple_of(p * 256 + 128 * h, 128), 128)] = qp * own[h] + extra
        scale = jnp.where(lane < 64, inverses[0], inverses[1])
        ctx_ref[0, :, cols] = (ctx * scale).astype(BF16)
        return 0

    lax.fori_loop(0, PAIRS, pair, 0)
    hidden = x + dot(ctx_ref[0], wo_ref[...]) + row_of(vec_ref, B_OUT)
    hid_ref[0] = hidden
    scaled, _ = norm_parts(hidden)
    n2_ref[0] = (scaled * row_of(vec_ref, GAIN_2) + row_of(vec_ref, SHIFT_2)).astype(BF16)


def whole(shape):
    return pl.BlockSpec(shape, lambda *_: (0,) * len(shape), pipeline_mode=pl.Buffered(1))


def strip_block(cols):
    return pl.BlockSpec((1, SLOTS, cols), lambda s, *_: (s, 0, 0))


def strips_of(cols, dtype):
    return jax.ShapeDtypeStruct((STRIPS, SLOTS, cols), dtype)


def attend(at, lengths, patches, got, cotangent, got_cot, vec, wq, wk, wv, wo):
    mat = whole((D, D))
    mine = pl.BlockSpec((1, HALF, D), lambda s, at_ref, *_: (STRIPS * at_ref[0] + s, 0, 0))
    half = pl.BlockSpec((1, HALF, D), lambda s, *_: (s, 0, 0))
    return call(
        attend_kernel,
        [at, lengths, far(patches), got, far(cotangent), got_cot, vec, far(wq), far(wk), far(wv), far(wo)],
        [mine, half, mine, half, whole((VECTORS, D)), mat, mat, mat, mat],
        [],
        prefetch=2,
        grid=(STRIPS,),
        out_specs=[strip_block(D), strip_block(2 * D)] + [strip_block(D)] * 7,
        scratch_shapes=[pltpu.VMEM((SLOTS, D), BF16)],
        out_shape=[pltpu.HBM((STRIPS, SLOTS, D), BF16), pltpu.HBM((STRIPS, SLOTS, 2 * D), BF16)]
        + [pltpu.HBM((STRIPS, SLOTS, D), BF16)] * 3
        + [pltpu.HBM((STRIPS, SLOTS, D), F32), pltpu.VMEM((STRIPS, SLOTS, D), BF16)]
        + [pltpu.HBM((STRIPS, SLOTS, D), BF16), pltpu.VMEM((STRIPS, SLOTS, D), BF16)],
        micros=28,
        mib=30,
        name="attend",
    )


def mlp_kernel(
    base, steps, which, at_ref, n2_ref, cot_ref, up_ref, dn_ref, vec_ref, acc_in_ref, *rest
):
    first, last = base == 0, (base + steps) * FSTEP == FF
    into = base % PIECE_STEPS
    gn_in_ref, rest = (None, rest) if first else (rest[0], rest[1:])
    rest = rest[2:] if into else rest
    keep_ref, send_ref, gn_ref, gbup_ref = rest[:4]
    acc_ref, outs, (a_scr, g_scr) = rest[4], rest[5:-2], rest[-2:]
    step = pl.program_id(0)

    @pl.when(step == 0)
    def _():
        if first:
            acc_ref[...] = acc_in_ref[...] + row_of(vec_ref, B_DOWN)
            gn_ref[...] = jnp.zeros_like(gn_ref)

    up, down = up_ref[...], dn_ref[...]
    bias = vec_ref[pl.ds(B_UP + base + step, 1)]
    sums = None
    for r in range(0, ROWS, SLOTS):
        rows = slice(r, r + SLOTS)
        u = dot(n2_ref[rows], up) + bias
        grad_active = dot_bt(cot_ref[rows], down)
        active, slope = gelu_parts(u)
        active = active.astype(BF16)
        grad_upper = (grad_active * slope).astype(BF16)
        a_scr[rows] = active
        g_scr[rows] = grad_upper
        acc_ref[rows] += dot(active, down)
        gn_ref[rows] += dot_bt(grad_upper, up)
        part = jnp.sum(grad_upper.astype(F32), axis=0, keepdims=True)
        sums = part if sums is None else sums + part
    gbup_ref[0] = sums
    grad_down = dot_at(a_scr[...], cot_ref[...]).astype(BF16)
    grad_up = dot_at(n2_ref[...], g_scr[...]).astype(BF16)
    core, place = at_ref[0], at_ref[which]
    chunk, rows_up = FCALL // 16, D // 16
    per_step = FSTEP // chunk
    part = into + step

    def put(down_ref, up_out_ref):
        for i in range(per_step):
            down_ref[(part * per_step + i) ^ place] = grad_down[i * chunk : (i + 1) * chunk]
        for i in range(16):
            rows = pl.ds(pl.multiple_of(part * rows_up, 16), rows_up)
            up_out_ref[i ^ place, rows] = grad_up[i * rows_up : (i + 1) * rows_up]

    @pl.when(core == 0)
    def _():
        put(keep_ref, send_ref)

    @pl.when(core == 1)
    def _():
        put(send_ref, keep_ref)

    if last:
        @pl.when(step == steps - 1)
        def _():
            for s in range(STRIPS):
                for ref, c in zip(outs, (core, 1 - core)):
                    rows = pl.ds(pl.multiple_of(SLOTS * s + HALF * c, 16), HALF)
                    ref[s] = acc_ref[rows].astype(BF16)


def mlp(base, steps, which, at, n2, cot, w_up, w_down, vec, acc, gn, piece, after):
    first, last = base == 0, (base + steps) * FSTEP == FF
    shape = (16, FCALL // 16, D)
    rows, near = whole((ROWS, D)), pl.BlockSpec(memory_space=pltpu.VMEM)
    in_specs = [
        near, near,
        pl.BlockSpec((D, FSTEP), lambda s, *_: (0, base + s)),
        pl.BlockSpec((FSTEP, D), lambda s, *_: (base + s, 0)),
        whole((VECTORS, D)), rows if first else near,
    ]
    operands = [at, n2, cot, far(w_up), far(w_down), vec, far(acc) if first else acc]
    aliases = {}
    if not first:
        in_specs.append(near)
        operands.append(gn)
        aliases = {6: 4, 7: 2}
    if piece:
        in_specs += [near, near]
        aliases |= {len(operands): 0, len(operands) + 1: 1}
        operands += piece
    kept = pltpu.VMEM(shape, BF16)
    halves = [jax.ShapeDtypeStruct((STRIPS, HALF, D), BF16)] * 2
    return call(
        functools.partial(mlp_kernel, base, steps, which), operands, in_specs, after,
        prefetch=1,
        grid=(steps,),
        out_specs=[near, near, near, pl.BlockSpec((1, 1, FSTEP), lambda s, *_: (s, 0, 0)), near]
        + ([whole((STRIPS, HALF, D))] * 2 if last else []),
        scratch_shapes=[pltpu.VMEM((ROWS, FSTEP), BF16)] * 2,
        out_shape=[kept, kept, pltpu.VMEM((ROWS, D), F32), jax.ShapeDtypeStruct((steps, 1, FSTEP), F32),
                   pltpu.VMEM((ROWS, D), F32)] + (halves if last else []),
        input_output_aliases=aliases,
        micros=12 * steps,
        mib=26,
        name="mlp",
    )


def mid_kernel(
    which, at_ref, gn_ref, hid_ref, cot_ref, ctx_ref, wo_ref, vec_ref,
    gh_ref, dctx_ref, gwo_ref, sums_ref, acc_scr,
):
    strip = pl.program_id(0)
    grad = gn_ref[0]
    cot = cot_ref[0].astype(F32)
    scaled, rstd = norm_parts(hid_ref[0])
    t = grad * row_of(vec_ref, GAIN_2)
    cross = jnp.mean(t * scaled, axis=-1, keepdims=True)
    grad_hidden = cot + rstd * (t - jnp.mean(t, axis=-1, keepdims=True) - scaled * cross)
    grad_attn = grad_hidden.astype(BF16)
    gh_ref[0] = grad_attn
    dctx_ref[0] = dot_bt(grad_attn, wo_ref[...]).astype(BF16)
    grad_out = dot_at(ctx_ref[0], grad_attn)
    sums = [
        jnp.sum(grad * scaled, axis=0, keepdims=True),
        jnp.sum(grad, axis=0, keepdims=True),
        jnp.sum(grad_attn.astype(F32), axis=0, keepdims=True),
        jnp.sum(cot, axis=0, keepdims=True),
    ]

    @pl.when(strip == 0)
    def _():
        acc_scr[...] = grad_out
        for i, value in enumerate(sums):
            sums_ref[i : i + 1] = value

    @pl.when(strip > 0)
    def _():
        total = (acc_scr[...] + grad_out).astype(BF16)
        for i in range(16):
            gwo_ref[i ^ at_ref[which]] = total[i * 48 : (i + 1) * 48]
        for i, value in enumerate(sums):
            sums_ref[i : i + 1] += value


def middle(which, at, gn, hid, cot, ctx, wo, vec, after):
    return call(
        functools.partial(mid_kernel, which), [at, gn, far(hid), cot, far(ctx), far(wo), vec],
        [strip_block(D)] * 4 + [whole((D, D)), whole((VECTORS, D))], after,
        prefetch=1,
        grid=(STRIPS,),
        out_specs=[strip_block(D), strip_block(D), whole((16, 48, D)), whole((8, D))],
        scratch_shapes=[pltpu.VMEM((D, D), F32)],
        out_shape=[pltpu.HBM((STRIPS, SLOTS, D), BF16)] * 2
        + [jax.ShapeDtypeStruct((16, 48, D), BF16), jax.ShapeDtypeStruct((8, D), F32)],
        micros=10,
        mib=22,
        name="middle",
    )


def back_kernel(
    which, at_ref, len_ref, qa_ref, k_ref, v_ref, dctx_ref, ctx_ref, n1_ref,
    grads_ref, d_ref, sums_ref, acc_scr,
):
    d_scr = d_ref.at[0]
    strip = pl.program_id(0)
    lane = lane_iota()
    own = [half_mask(lane, h) for h in (0, 1)]
    length = len_ref[STRIPS * at_ref[0] + strip]
    kx = [key_extra(lane, length, h) for h in (0, 1)]
    vx = [
        jnp.where((lane > 64 * (1 - h)) & (lane < 64 * (1 - h) + 4), 1.0, 0.0).astype(BF16)
        for h in (0, 1)
    ]
    for p in range(GROUP_PAIRS):
        cols = slice(p * 128, p * 128 + 128)
        kp, vp, dp, cp = k_ref[0, :, cols], v_ref[0, :, cols], dctx_ref[0, :, cols], ctx_ref[0, :, cols]
        product = dp.astype(F32) * cp.astype(F32)
        dq, dk, dv = [], [], []
        for h in (0, 1):
            query = qa_ref[0, :, p * 256 + 128 * h : p * 256 + 128 * h + 128]
            inner = jnp.sum(product * own[h].astype(F32), axis=-1, keepdims=True)
            grad = dp * own[h] + pieces_extra(lane, -inner, h, 0.0)
            probs = jnp.exp(dot_bt(kp * own[h] + kx[h], query))
            grad_scores = (probs * dot_bt(vp * own[h] + vx[h], grad)).astype(BF16)
            dv.append(dot(probs.astype(BF16), dp))
            dk.append(dot(grad_scores, query))
            dq.append(dot_at(grad_scores, kp))
        low = lane < 64
        d_scr[:, cols] = (jnp.where(low, dq[0], dq[1]) * (HEAD_DIM**-0.5)).astype(BF16)
        d_scr[:, GCOLS + p * 128 : GCOLS + p * 128 + 128] = jnp.where(low, dk[0], dk[1]).astype(BF16)
        d_scr[:, 2 * GCOLS + p * 128 : 2 * GCOLS + p * 128 + 128] = jnp.where(low, dv[0], dv[1]).astype(BF16)
    d_all = d_scr[...]
    grad = dot_at(n1_ref[0], d_all)
    sums = jnp.sum(d_all.astype(F32), axis=0, keepdims=True)

    @pl.when(strip == 0)
    def _():
        acc_scr[...] = grad
        sums_ref[...] = sums

    @pl.when(strip > 0)
    def _():
        total = (acc_scr[...] + grad).astype(BF16)
        for i in range(16):
            grads_ref[i ^ at_ref[which]] = total[i * 48 : (i + 1) * 48]
        sums_ref[...] += sums


def attend_back(group, which, at, lengths, qa, k, v, dctx, ctx, n1, after):
    def cols(width):
        return pl.BlockSpec((1, SLOTS, width), lambda s, *_: (s, 0, group))

    return call(
        functools.partial(back_kernel, which),
        [at, lengths] + [far(o) for o in (qa, k, v, dctx, ctx, n1)],
        [cols(2 * GCOLS)] + [cols(GCOLS)] * 4 + [strip_block(D)], after,
        prefetch=2,
        grid=(STRIPS,),
        out_specs=[whole((16, 48, D)), strip_block(3 * GCOLS), whole((1, 3 * GCOLS))],
        scratch_shapes=[pltpu.VMEM((D, 3 * GCOLS), F32)],
        out_shape=[jax.ShapeDtypeStruct((16, 48, D), BF16), pltpu.HBM((STRIPS, SLOTS, 3 * GCOLS), BF16),
                   jax.ShapeDtypeStruct((1, 3 * GCOLS), F32)],
        micros=12,
        mib=18,
        name="attend_back",
    )


def end_kernel(
    at_ref, d0_ref, d1_ref, d2_ref, wq_ref, wk_ref, wv_ref, x_ref, gh_ref, vec_ref, mid_ref, s0_ref, s1_ref, s2_ref,
    up0_ref, up1_ref, up2_ref, own_ref, other_ref, small_ref, acc_scr, gp_scr,
):
    strip = pl.program_id(0)
    grad = None
    for g, d_ref in enumerate((d0_ref, d1_ref, d2_ref)):
        for i, w_ref in enumerate((wq_ref, wk_ref, wv_ref)):
            part = dot_bt(d_ref[0, :, i * GCOLS : (i + 1) * GCOLS], w_ref[:, g * GCOLS : (g + 1) * GCOLS])
            grad = part if grad is None else grad + part
    scaled, rstd = norm_parts(x_ref[0].astype(F32))
    t = grad * row_of(vec_ref, GAIN_1)
    cross = jnp.mean(t * scaled, axis=-1, keepdims=True)
    grad_in = rstd * (t - jnp.mean(t, axis=-1, keepdims=True) - scaled * cross)
    gp_scr[...] = (gh_ref[0].astype(F32) + grad_in).astype(BF16)
    core = at_ref[0]
    own_ref[0] = gp_scr[pl.ds(pl.multiple_of(core * HALF, 16), HALF)]
    other_ref[0] = gp_scr[pl.ds(pl.multiple_of((1 - core) * HALF, 16), HALF)]
    sums = [jnp.sum(grad * scaled, axis=0, keepdims=True), jnp.sum(grad, axis=0, keepdims=True)]

    @pl.when(strip == 0)
    def _():
        acc_scr[0:1], acc_scr[1:2] = sums

    @pl.when(strip > 0)
    def _():
        acc_scr[0:1] += sums[0]
        acc_scr[1:2] += sums[1]
        for g, s_ref in enumerate((s0_ref, s1_ref, s2_ref)):
            cols = slice(g * GCOLS, (g + 1) * GCOLS)
            acc_scr[2:3, cols] = s_ref[:, :GCOLS]
            acc_scr[3:4, cols] = s_ref[:, 2 * GCOLS :]
        acc_scr[4:8] = mid_ref[0:4]
        ups = [up0_ref[0], up0_ref[1], up1_ref[0], up2_ref[0]]
        for i, value in enumerate(ups):
            acc_scr[8 + i : 9 + i] = value
        acc_scr[12:16] = jnp.zeros((4, D), F32)
        small_ref[...] = acc_scr[...].astype(BF16)


def end(at, ds, wq, wk, wv, x, gh, vec, mid, sums, ups, after):
    half = pl.BlockSpec((1, HALF, D), lambda s, *_: (s, 0, 0))
    small = [mid, *sums, *ups]
    return call(
        end_kernel, [at, *(far(d) for d in ds), far(wq), far(wk), far(wv), far(x), far(gh), vec, *small],
        [strip_block(D)] * 3 + [whole((D, D))] * 3 + [strip_block(D)] * 2 + [whole((VECTORS, D))]
        + [whole(v.shape) for v in small], after,
        prefetch=1,
        grid=(STRIPS,),
        out_specs=[half, half, whole((SMALL, D))],
        scratch_shapes=[pltpu.VMEM((SMALL, D), F32), pltpu.VMEM((SLOTS, D), BF16)],
        out_shape=[jax.ShapeDtypeStruct((STRIPS, HALF, D), BF16)] * 2 + [jax.ShapeDtypeStruct((SMALL, D), BF16)],
        micros=9,
        mib=24,
        name="end",
    )


def back_in_place_kernel(at_ref, own_ref, got_ref, out_ref):
    mine = (pl.program_id(0) // STRIPS) == at_ref[0]

    @pl.when(mine)
    def _():
        out_ref[...] = own_ref[...]

    @pl.when(jnp.logical_not(mine))
    def _():
        out_ref[...] = got_ref[...]


def back_in_place(at, own, other, after):
    got = swap(other, "seq", 1, 2)
    block = (1, HALF, D)
    spec = pl.BlockSpec(block, lambda i, *_: (lax.rem(i, STRIPS), 0, 0))
    return call(
        back_in_place_kernel, [at, own, got], [spec, spec], after,
        prefetch=1,
        grid=(2 * STRIPS,),
        out_specs=pl.BlockSpec(block, lambda i, *_: (i, 0, 0)),
        out_shape=pltpu.HBM((2 * STRIPS, HALF, D), BF16),
        micros=2,
        mib=8,
        name="in_place",
    )


WIDE = 4


def crossed(i, cross):
    return i // 2 + 2 * lax.rem(i, 2) if cross else i


def widen_mlp_kernel(which, at_ref, mine_ref, other_ref, *rest):
    down_ref, up_ref = rest[-2:]
    swapped = at_ref[0] == 1
    place = lax.rem(at_ref[which], WIDE)
    for i in range(WIDE):
        mine, other = mine_ref[i ^ place], other_ref[i ^ place]
        down_ref[i * 96 : i * 96 + 96] = jnp.where(swapped, other, mine).astype(F32)
        up = jnp.where(swapped, mine, other).astype(F32)
        up_ref[i * 48 : i * 48 + 48, :D] = up[:48]
        up_ref[i * 48 : i * 48 + 48, D:] = up[48:]


def widen_mlp(part, at, p, given, after):
    which = p.which
    block = pl.BlockSpec(
        (WIDE, FCALL // 16, D), lambda i, at_ref: (crossed(i, p.cross) ^ (at_ref[which] // WIDE), 0, 0)
    )
    given = list(given)
    return call(
        functools.partial(widen_mlp_kernel, which), [at, p.total, p.got] + given,
        [block, block] + [pl.BlockSpec(memory_space=pl.ANY)] * len(given), after,
        prefetch=1,
        grid=(16 // WIDE,),
        out_specs=[
            pl.BlockSpec((WIDE * FCALL // 16, D), lambda i, *_: (16 // WIDE * part + i, 0)),
            pl.BlockSpec((WIDE * D // 16, FCALL), lambda i, *_: (i, part)),
        ],
        out_shape=[jax.ShapeDtypeStruct((FF, D), F32), jax.ShapeDtypeStruct((D, FF), F32)],
        input_output_aliases={3: 0, 4: 1} if given else {},
        micros=4,
        mib=12,
        name="widen_mlp",
    )


def widen_attn_kernel(w0, w1, cross1, at_ref, m0_ref, o0_ref, m1_ref, o1_ref, out_ref, q_ref, k_ref, v_ref, small_ref):
    swapped = at_ref[0] == 1
    first, second = lax.rem(at_ref[w0], WIDE), lax.rem(at_ref[w1], WIDE)
    block1 = crossed(pl.program_id(0), cross1) ^ (at_ref[w1] // WIDE)
    for i in range(WIDE):
        rows = slice(i * 48, i * 48 + 48)
        m0, o0 = m0_ref[i ^ first].astype(F32), o0_ref[i ^ first].astype(F32)
        at1 = pl.ds(pl.multiple_of((block1 * WIDE + (i ^ second)) * 48, 16), 48)
        m1, o1 = m1_ref[at1].astype(F32), o1_ref[at1].astype(F32)
        out_ref[rows] = jnp.where(swapped, o0, m0)
        blocks = (jnp.where(swapped, m0, o0), jnp.where(swapped, o1, m1), jnp.where(swapped, m1, o1))
        for g, block in enumerate(blocks):
            cols = slice(g * GCOLS, (g + 1) * GCOLS)
            q_ref[rows, cols] = block[:, :GCOLS]
            k_ref[rows, cols] = block[:, GCOLS : 2 * GCOLS]
            v_ref[rows, cols] = block[:, 2 * GCOLS :]
    small_ref[...] = m1_ref[16 * 48 :].astype(F32) + o1_ref[16 * 48 :].astype(F32)


def widen_attn(at, p0, p1, after):
    w0, w1 = p0.which, p1.which
    block = pl.BlockSpec((WIDE, 48, D), lambda i, at_ref: (crossed(i, p0.cross) ^ (at_ref[w0] // WIDE), 0, 0))
    rows = whole((16 * 48 + SMALL, D))
    return call(
        functools.partial(widen_attn_kernel, w0, w1, p1.cross), [at, p0.total, p0.got, p1.total, p1.got], [block, block, rows, rows], after,
        prefetch=1,
        grid=(16 // WIDE,),
        out_specs=[pl.BlockSpec((WIDE * 48, D), lambda i, *_: (i, 0))] * 4 + [whole((SMALL, D))],
        out_shape=[jax.ShapeDtypeStruct((D, D), F32)] * 4 + [jax.ShapeDtypeStruct((SMALL, D), F32)],
        micros=4,
        mib=16,
        name="widen_attn",
    )


def swap(value, axis, bit, size):
    return lax.ppermute(value, axis, [(i, i ^ bit) for i in range(size)])


TAIL = (
    "b", "end", "1", "0", "a", "b", "place", "b", "a", "1", "0", "b", "a", "0", "1", "a",
    "b", "a", "1", "b", "b", "0", "1", "a", "wide", "b", "a", "b", "1",
)


class Sum:
    def __init__(self, order, back, dp, keep=None, send=None, pick=None):
        self.keep, self.send, self.pick, self.small = keep, send, pick, None
        rest = [1 << i for i in range(4, dp.bit_length() - 1)]
        hops = [("seq", 1, 2, "half")] + [("dp", b, dp, "half") for b in order]
        hops += [("dp", b, dp, "whole") for b in rest]
        hops += [("dp", b, dp, "join") for b in back] + [("seq", 1, 2, "pair")]
        self.hops, self.total, self.got = hops, None, None
        self.which = 1 if back[-1] == 1 else 2
        self.cross = back[-1] != order[0]

    def start(self):
        axis, bit, size, kind = self.hops[0]
        self.got = swap(self.send if kind == "half" else self.total, axis, bit, size)


def merge_kernel(kinds, *refs):
    at_ref, refs = refs[0], refs[1:]
    outs = refs[sum(3 if kind == "load" else 2 for kind in kinds) :]
    for kind in kinds:
        (a, b), refs = refs[:2], refs[2:]
        if kind == "pick":
            keep, send = outs[:2]

            @pl.when(at_ref[0] == 0)
            def _():
                keep[...], send[...] = a[...], b[...]

            @pl.when(at_ref[0] != 0)
            def _():
                keep[...], send[...] = b[...], a[...]

        elif kind == "split":
            half = a.shape[0] // 2
            outs[0][...] = a[:half] + b[:half]
            outs[1][...] = a[half:] + b[half:]
        elif kind == "add":
            outs[0][...] = a[...] + b[...]
        elif kind == "load":
            rows = a.shape[1]
            outs[0][:rows] = a[0] + b[0]
            outs[0][rows:] = refs[0][...]
            refs = refs[1:]
        elif kind == "join":
            half = a.shape[0]
            outs[0][:half] = a[...]
            outs[0][half:] = b[...]
        else:
            rows = a.shape[0] - SMALL
            outs[0][:rows], outs[0][rows : 2 * rows] = a[:rows], b[:rows]
            outs[0][2 * rows :] = a[rows:] + b[rows:]
        outs = outs[2 if kind in ("pick", "split") else 1 :]


def merge(at, pieces, after):
    kinds, operands, shapes = [], [], []
    for p in pieces:
        if p.pick:
            kind, args = "pick", list(p.pick)
        else:
            kind = p.hops.pop(0)[3]
            args = [p.keep if kind == "half" else p.total, p.got]
            if kind == "half":
                kind = "split" if p.hops[0][3] == "half" else "add"
            elif kind == "whole":
                kind = "add"
            if p.small is not None and kind == "add" and p.hops[0][3] == "join":
                kind, args = "load", args + [p.small]
            elif p.small is not None and kind == "join":
                kind = "carry"
        n, tail = args[0].shape[0], args[0].shape[1:]
        n = {"pick": [n, n], "split": [n // 2, n // 2], "add": [n], "join": [2 * n], "carry": [2 * n - SMALL],
             "load": [1]}[kind]
        kinds.append(kind)
        operands += args
        shapes.append([(tail[0] + SMALL, D)] if kind == "load" else [(m,) + tail for m in n])
    flat = [shape for group in shapes for shape in group]
    size = sum(2 * v.size for v in operands) + sum(2 * D * (s[0] * s[1] // D if len(s) == 2 else s[0] * s[1]) for s in flat)
    outs = list(call(
        functools.partial(merge_kernel, kinds), [at] + operands, [whole(v.shape) for v in operands], after,
        prefetch=1,
        grid=(1,),
        out_specs=[whole(shape) for shape in flat],
        out_shape=[jax.ShapeDtypeStruct(shape, BF16) for shape in flat],
        micros=2,
        mib=4 + (size >> 20),
        name="merge",
    ))
    made = list(outs)
    for p, kind in zip(pieces, kinds):
        p.pick = None
        if kind in ("pick", "split"):
            p.keep, p.send = outs[:2]
            outs = outs[2:]
        else:
            p.total, outs = outs[0], outs[1:]
        p.start()
    return made


def local(
    dp, patches, lengths, gain_one, shift_one, w_query, b_query, w_key, w_value, b_value, w_out, b_out,
    gain_two, shift_two, w_up, b_up, w_down, b_down, cotangent,
):
    core, block = lax.axis_index("seq"), lax.axis_index("dp")
    x_first, y_first = (1, 2, 4, 8), (2, 1, 4, 8)

    def place_of(order):
        return sum(jnp.where((block & bit) != 0, 8 >> i, 0) for i, bit in enumerate(order))

    at = jnp.stack([core, place_of(x_first), place_of(y_first)]).astype(jnp.int32)
    foreign = lambda v: lax.dynamic_slice(v, (STRIPS * (1 - core), 0, 0), (STRIPS, HALF, D))
    got = swap(foreign(patches), "seq", 1, 2)
    got_cot = swap(foreign(cotangent), "seq", 1, 2)
    vectors = (gain_one, shift_one, b_query, b_value, b_out, gain_two, shift_two, b_down, b_up)
    vec = jnp.concatenate(vectors).reshape(VECTORS, D)
    n1, qa, k, v, ctx, hid, n2, x, cot = attend(
        at, lengths, patches, got, cotangent, got_cot, vec, w_query, w_key, w_value, w_out
    )
    flat = lambda v: v.reshape(ROWS, D)
    shared = (at, flat(n2), flat(cot), w_up, w_down, vec)
    keep, send, gn, up_0, acc = mlp(0, 2, 1, *shared, flat(hid), None, None, [])
    m0 = Sum(x_first, Y_LAST, dp, keep, send)
    m0.start()
    keep, send, gn, up_1, acc = mlp(2, 1, 1, *shared, acc, gn, None, [])
    made = merge(at, [m0], [gn])
    keep, send, gn, up_2, _, out_own, out_other = mlp(3, 1, 1, *shared, acc, gn, (keep, send), made)
    m1 = Sum(x_first, Y_LAST, dp, keep, send)
    m1.start()
    gh, dctx, g_out, sums_mid = middle(1, at, gn.reshape(STRIPS, SLOTS, D), hid, cot, ctx, w_out, vec, [send])
    made = merge(at, [m0, m1], [g_out])
    back = (at, lengths, qa, k, v, dctx, ctx, n1)
    grads_0, d_0, sums_0 = attend_back(0, 1, *back, made)
    a0 = Sum(x_first, X_LAST, dp, pick=(g_out, grads_0))
    made = merge(at, [m0, a0], [grads_0])
    output = back_in_place(at, out_own, out_other, made)
    grads_1, d_1, sums_1 = attend_back(1, 1, *back, made)
    made = merge(at, [m0, m1, a0], [grads_1])
    grads_2, d_2, sums_2 = attend_back(2, 1, *back, made + [output])
    a1 = Sum(x_first, X_LAST, dp, pick=(grads_1, grads_2))
    made = merge(at, [m0, m1, a0, a1], [grads_2])
    pieces = {"0": m0, "1": m1, "a": a0, "b": a1}
    for turn in TAIL:
        if turn == "end":
            gp_own, gp_other, a1.small = end(
                at, (d_0, d_1, d_2), w_query, w_key, w_value, x, gh, vec, sums_mid, (sums_0, sums_1, sums_2),
                (up_0, up_1, up_2), made,
            )
            for bit in range(4, dp.bit_length() - 1):
                a1.small = a1.small + swap(a1.small, "dp", 1 << bit, dp)
            made = [a1.small]
        elif turn == "place":
            grad_patches = back_in_place(at, gp_own, gp_other, made)
            made = [grad_patches]
        elif turn == "wide":
            given = widen_mlp(0, at, m0, (), made)
            made = [given[0]]
        else:
            made = merge(at, [pieces[c] for c in turn], made)
    for p in pieces.values():
        while len(p.hops) > 1:
            made = merge(at, [p], made)
    g_out, g_query, g_key, g_value, small = widen_attn(at, a0, a1, [])
    g_down, g_up = widen_mlp(1, at, m1, given, [])
    small = small.reshape(-1)
    vecs = [small[i * D : (i + 1) * D] for i in range(8)]
    g_bup = small[8 * D : 8 * D + FF]
    return (
        output, grad_patches, vecs[0], vecs[1], g_query, vecs[2], g_key, g_value, vecs[3], g_out, vecs[6],
        vecs[4], vecs[5], g_up, g_bup, g_down, vecs[7],
    )


def solution(mesh):
    dp = mesh.shape["dp"]
    rows, rep = P("dp", "seq", None), P()
    return jax.shard_map(
        functools.partial(local, dp),
        mesh=mesh,
        in_specs=(rows, P("dp")) + (rep,) * 15 + (rows,),
        out_specs=(rows, rows) + (rep,) * 15,
        check_vma=False,
    )
```

```python
import functools

import jax
import jax.numpy as jnp
from jax import lax
from jax.experimental import pallas as pl
from jax.experimental.pallas import tpu as pltpu
from jax.sharding import PartitionSpec as P

F32, BF16 = jnp.float32, jnp.bfloat16
D, HEADS, HEAD_DIM, FF, SLOTS = 768, 12, 64, 3072, 544
X_LAST, Y_LAST = (8, 4, 2, 1), (8, 4, 1, 2)
STRIPS = 2
ROWS = STRIPS * SLOTS
PAIRS = HEADS // 2
EPS = 1e-06
MASKED = -1e30
GROUPS = 3
GROUP_PAIRS = PAIRS // GROUPS
GCOLS = D // GROUPS
HALF = SLOTS // 2
FSTEP = 768
PIECE_STEPS = 2
FCALL = FSTEP * PIECE_STEPS
GAIN_1, SHIFT_1, B_QUERY, B_VALUE, B_OUT, GAIN_2, SHIFT_2, B_DOWN, B_UP = range(9)
VECTORS = B_UP + FF // D
SMALL = 16


def params(mib):
    return pltpu.CompilerParams(vmem_limit_bytes=mib << 20, dimension_semantics=("arbitrary",))


def far(value):
    return pltpu.with_memory_space_constraint(value, pltpu.HBM)


def cost(micros):
    return pl.CostEstimate(flops=int(micros * 1.15e10), bytes_accessed=0, transcendentals=0)


def call(kernel, operands, in_specs, after, prefetch=0, micros=10, mib=16, **kw):
    after = [v for v in after if v is not None]
    count = len(after)
    scalars = operands[:prefetch]

    def body(*refs):
        n = prefetch + len(in_specs)
        kernel(*refs[:n], *refs[n + count :])

    spec = pltpu.PrefetchScalarGridSpec(
        num_scalar_prefetch=prefetch,
        grid=kw.pop("grid"),
        in_specs=list(in_specs) + [pl.BlockSpec(memory_space=pl.ANY)] * count,
        out_specs=kw.pop("out_specs"),
        scratch_shapes=kw.pop("scratch_shapes", []),
    )
    return pl.pallas_call(body, grid_spec=spec, compiler_params=params(mib), cost_estimate=cost(micros), **kw)(
        *operands, *after
    )


def dot(a, b):
    return lax.dot_general(a, b, (((1,), (0,)), ((), ())), preferred_element_type=F32)


def dot_bt(a, b):
    return lax.dot_general(a, b, (((1,), (1,)), ((), ())), preferred_element_type=F32)


def dot_at(a, b):
    return lax.dot_general(a, b, (((0,), (0,)), ((), ())), preferred_element_type=F32)


def norm_parts(values):
    centre = jnp.mean(values, axis=-1, keepdims=True)
    centred = values - centre
    spread = jnp.mean(centred * centred, axis=-1, keepdims=True)
    rstd = lax.rsqrt(spread + EPS)
    return centred * rstd, rstd


def gelu_parts(u):
    t = 1.0 / (1.0 + (0.3275911 * 0.7071067811865476) * jnp.abs(u))
    e = jnp.exp(-0.5 * u * u)
    poly = 0.5 * 1.061405429 * t + 0.5 * -1.453152027
    poly = poly * t + 0.5 * 1.421413741
    poly = poly * t + 0.5 * -0.284496736
    poly = poly * t + 0.5 * 0.254829592
    tail = poly * t * e
    cdf = jnp.where(u >= 0, 1.0 - tail, tail)
    return u * cdf, cdf + u * (e * 0.3989422804014327)


def split3(x):
    hi = x.astype(BF16).astype(F32)
    rest = x - hi
    mid = rest.astype(BF16).astype(F32)
    return hi, mid, rest - mid


def lane_iota():
    return lax.broadcasted_iota(jnp.int32, (SLOTS, 128), 1)


def half_mask(lane, h):
    return jnp.where((lane >= 64 * h) & (lane < 64 * h + 64), 1.0, 0.0).astype(BF16)


def key_extra(lane, length, h):
    first = 64 * (1 - h)
    row = lax.broadcasted_iota(jnp.int32, (SLOTS, 128), 0)
    bias = jnp.where(row < length, 0.0, MASKED)
    ones = (lane > first) & (lane < first + 4)
    return jnp.where(lane == first, bias, jnp.where(ones, 1.0, 0.0)).astype(BF16)


def pieces_extra(lane, column, h, lead):
    first = 64 * (1 - h)
    hi, mid, low = split3(column)
    out = jnp.where(lane == first + 3, low, jnp.where(lane == first, lead, 0.0))
    out = jnp.where(lane == first + 2, mid, out)
    return jnp.where(lane == first + 1, hi, out).astype(BF16)


def row_of(ref, i):
    return ref[i : i + 1]


def attend_kernel(
    at_ref, len_ref, own_ref, got_ref, own_cot_ref, got_cot_ref, vec_ref, wq_ref, wk_ref, wv_ref, wo_ref,
    n1_ref, qa_ref, k_ref, v_ref, ctx_ref, hid_ref, n2_ref, x_ref, cot_ref, q_scr,
):
    core = at_ref[0]
    own_rows = pl.ds(pl.multiple_of(core * HALF, 16), HALF)
    got_rows = pl.ds(pl.multiple_of((1 - core) * HALF, 16), HALF)
    x_ref[0, own_rows], x_ref[0, got_rows] = own_ref[0], got_ref[0]
    cot_ref[0, own_rows], cot_ref[0, got_rows] = own_cot_ref[0], got_cot_ref[0]
    x = x_ref[0].astype(F32)
    scaled, _ = norm_parts(x)
    n1 = (scaled * row_of(vec_ref, GAIN_1) + row_of(vec_ref, SHIFT_1)).astype(BF16)
    n1_ref[0] = n1
    queries = (dot(n1, wq_ref[...]) + row_of(vec_ref, B_QUERY)).astype(BF16)
    q_scr[...] = (queries.astype(F32) * (HEAD_DIM**-0.5)).astype(BF16)
    k_ref[0] = dot(n1, wk_ref[...]).astype(BF16)
    v_ref[0] = (dot(n1, wv_ref[...]) + row_of(vec_ref, B_VALUE)).astype(BF16)
    length = len_ref[STRIPS * core + pl.program_id(0)]
    lane = lane_iota()
    own = [half_mask(lane, h) for h in (0, 1)]
    kx = [key_extra(lane, length, h) for h in (0, 1)]

    def pair(p, _):
        cols = pl.ds(pl.multiple_of(p * 128, 128), 128)
        qp, kp, vp = q_scr[:, cols], k_ref[0, :, cols], v_ref[0, :, cols]
        ctx = None
        inverses = []
        for h in (0, 1):
            first = 64 * (1 - h)
            query = qp * own[h] + jnp.where(lane == first, 1.0, 0.0).astype(BF16)
            scores = dot_bt(query, kp * own[h] + kx[h])
            top = jnp.max(scores, axis=-1, keepdims=True)
            weights = jnp.exp(scores - top)
            total = jnp.sum(weights, axis=-1, keepdims=True)
            part = dot(weights.astype(BF16), vp * own[h])
            ctx = part if ctx is None else ctx + part
            inverses.append(1.0 / total)
            extra = pieces_extra(lane, -(top + jnp.log(total)), h, 1.0)
            qa_ref[0, :, pl.ds(pl.multiple_of(p * 256 + 128 * h, 128), 128)] = qp * own[h] + extra
        scale = jnp.where(lane < 64, inverses[0], inverses[1])
        ctx_ref[0, :, cols] = (ctx * scale).astype(BF16)
        return 0

    lax.fori_loop(0, PAIRS, pair, 0, unroll=2)
    hidden = x + dot(ctx_ref[0], wo_ref[...]) + row_of(vec_ref, B_OUT)
    hid_ref[0] = hidden
    scaled, _ = norm_parts(hidden)
    n2_ref[0] = (scaled * row_of(vec_ref, GAIN_2) + row_of(vec_ref, SHIFT_2)).astype(BF16)


def whole(shape):
    return pl.BlockSpec(shape, lambda *_: (0,) * len(shape), pipeline_mode=pl.Buffered(1))


def strip_block(cols):
    return pl.BlockSpec((1, SLOTS, cols), lambda s, *_: (s, 0, 0))


def strips_of(cols, dtype):
    return jax.ShapeDtypeStruct((STRIPS, SLOTS, cols), dtype)


def attend(at, lengths, patches, got, cotangent, got_cot, vec, wq, wk, wv, wo):
    mat = whole((D, D))
    mine = pl.BlockSpec((1, HALF, D), lambda s, at_ref, *_: (STRIPS * at_ref[0] + s, 0, 0))
    half = pl.BlockSpec((1, HALF, D), lambda s, *_: (s, 0, 0))
    return call(
        attend_kernel,
        [at, lengths, far(patches), got, far(cotangent), got_cot, vec, far(wq), far(wk), far(wv), far(wo)],
        [mine, half, mine, half, whole((VECTORS, D)), mat, mat, mat, mat],
        [],
        prefetch=2,
        grid=(STRIPS,),
        out_specs=[strip_block(D), strip_block(2 * D)] + [strip_block(D)] * 7,
        scratch_shapes=[pltpu.VMEM((SLOTS, D), BF16)],
        out_shape=[pltpu.HBM((STRIPS, SLOTS, D), BF16), pltpu.HBM((STRIPS, SLOTS, 2 * D), BF16)]
        + [pltpu.HBM((STRIPS, SLOTS, D), BF16)] * 3
        + [pltpu.HBM((STRIPS, SLOTS, D), F32), pltpu.VMEM((STRIPS, SLOTS, D), BF16)]
        + [pltpu.HBM((STRIPS, SLOTS, D), BF16), pltpu.VMEM((STRIPS, SLOTS, D), BF16)],
        micros=28,
        mib=44,
        name="attend",
    )


def mlp_kernel(
    base, steps, which, at_ref, n2_ref, cot_ref, up_ref, dn_ref, vec_ref, acc_in_ref, *rest
):
    first, last = base == 0, (base + steps) * FSTEP == FF
    into = base % PIECE_STEPS
    gn_in_ref, rest = (None, rest) if first else (rest[0], rest[1:])
    rest = rest[2:] if into else rest
    keep_ref, send_ref, gn_ref, gbup_ref = rest[:4]
    acc_ref, outs, (a_scr, g_scr) = rest[4], rest[5:-2], rest[-2:]
    step = pl.program_id(0)

    @pl.when(step == 0)
    def _():
        if first:
            acc_ref[...] = acc_in_ref[...] + row_of(vec_ref, B_DOWN)
            gn_ref[...] = jnp.zeros_like(gn_ref)

    up, down = up_ref[...], dn_ref[...]
    bias = vec_ref[pl.ds(B_UP + base + step, 1)]
    sums = None
    for r in range(0, ROWS, SLOTS):
        rows = slice(r, r + SLOTS)
        u = dot(n2_ref[rows], up) + bias
        grad_active = dot_bt(cot_ref[rows], down)
        active, slope = gelu_parts(u)
        active = active.astype(BF16)
        grad_upper = (grad_active * slope).astype(BF16)
        a_scr[rows] = active
        g_scr[rows] = grad_upper
        acc_ref[rows] += dot(active, down)
        gn_ref[rows] += dot_bt(grad_upper, up)
        part = jnp.sum(grad_upper.astype(F32), axis=0, keepdims=True)
        sums = part if sums is None else sums + part
    gbup_ref[0] = sums
    grad_down = dot_at(a_scr[...], cot_ref[...]).astype(BF16)
    grad_up = dot_at(n2_ref[...], g_scr[...]).astype(BF16)
    core, place = at_ref[0], at_ref[which]
    chunk, rows_up = FCALL // 16, D // 16
    per_step = FSTEP // chunk
    part = into + step

    def put(down_ref, up_out_ref):
        for i in range(per_step):
            down_ref[(part * per_step + i) ^ place] = grad_down[i * chunk : (i + 1) * chunk]
        for i in range(16):
            rows = pl.ds(pl.multiple_of(part * rows_up, 16), rows_up)
            up_out_ref[i ^ place, rows] = grad_up[i * rows_up : (i + 1) * rows_up]

    @pl.when(core == 0)
    def _():
        put(keep_ref, send_ref)

    @pl.when(core == 1)
    def _():
        put(send_ref, keep_ref)

    if last:
        @pl.when(step == steps - 1)
        def _():
            for s in range(STRIPS):
                for ref, c in zip(outs, (core, 1 - core)):
                    rows = pl.ds(pl.multiple_of(SLOTS * s + HALF * c, 16), HALF)
                    ref[s] = acc_ref[rows].astype(BF16)


def mlp(base, steps, which, at, n2, cot, w_up, w_down, vec, acc, gn, piece, after):
    first, last = base == 0, (base + steps) * FSTEP == FF
    shape = (16, FCALL // 16, D)
    rows, near = whole((ROWS, D)), pl.BlockSpec(memory_space=pltpu.VMEM)
    in_specs = [
        near, near,
        pl.BlockSpec((D, FSTEP), lambda s, *_: (0, base + s)),
        pl.BlockSpec((FSTEP, D), lambda s, *_: (base + s, 0)),
        whole((VECTORS, D)), rows if first else near,
    ]
    operands = [at, n2, cot, far(w_up), far(w_down), vec, far(acc) if first else acc]
    aliases = {}
    if not first:
        in_specs.append(near)
        operands.append(gn)
        aliases = {6: 4, 7: 2}
    if piece:
        in_specs += [near, near]
        aliases |= {len(operands): 0, len(operands) + 1: 1}
        operands += piece
    kept = pltpu.VMEM(shape, BF16)
    halves = [jax.ShapeDtypeStruct((STRIPS, HALF, D), BF16)] * 2
    return call(
        functools.partial(mlp_kernel, base, steps, which), operands, in_specs, after,
        prefetch=1,
        grid=(steps,),
        out_specs=[near, near, near, pl.BlockSpec((1, 1, FSTEP), lambda s, *_: (s, 0, 0)), near]
        + ([whole((STRIPS, HALF, D))] * 2 if last else []),
        scratch_shapes=[pltpu.VMEM((ROWS, FSTEP), BF16)] * 2,
        out_shape=[kept, kept, pltpu.VMEM((ROWS, D), F32), jax.ShapeDtypeStruct((steps, 1, FSTEP), F32),
                   pltpu.VMEM((ROWS, D), F32)] + (halves if last else []),
        input_output_aliases=aliases,
        micros=12 * steps,
        mib=26,
        name="mlp",
    )


def mid_kernel(
    which, at_ref, gn_ref, hid_ref, cot_ref, ctx_ref, wo_ref, vec_ref,
    gh_ref, dctx_ref, gwo_ref, sums_ref, acc_scr,
):
    strip = pl.program_id(0)
    grad = gn_ref[0]
    cot = cot_ref[0].astype(F32)
    scaled, rstd = norm_parts(hid_ref[0])
    t = grad * row_of(vec_ref, GAIN_2)
    cross = jnp.mean(t * scaled, axis=-1, keepdims=True)
    grad_hidden = cot + rstd * (t - jnp.mean(t, axis=-1, keepdims=True) - scaled * cross)
    grad_attn = grad_hidden.astype(BF16)
    gh_ref[0] = grad_attn
    dctx_ref[0] = dot_bt(grad_attn, wo_ref[...]).astype(BF16)
    grad_out = dot_at(ctx_ref[0], grad_attn)
    sums = [
        jnp.sum(grad * scaled, axis=0, keepdims=True),
        jnp.sum(grad, axis=0, keepdims=True),
        jnp.sum(grad_attn.astype(F32), axis=0, keepdims=True),
        jnp.sum(cot, axis=0, keepdims=True),
    ]

    @pl.when(strip == 0)
    def _():
        acc_scr[...] = grad_out
        for i, value in enumerate(sums):
            sums_ref[i : i + 1] = value

    @pl.when(strip > 0)
    def _():
        total = (acc_scr[...] + grad_out).astype(BF16)
        for i in range(16):
            gwo_ref[i ^ at_ref[which]] = total[i * 48 : (i + 1) * 48]
        for i, value in enumerate(sums):
            sums_ref[i : i + 1] += value


def middle(which, at, gn, hid, cot, ctx, wo, vec, after):
    return call(
        functools.partial(mid_kernel, which), [at, gn, far(hid), cot, far(ctx), far(wo), vec],
        [strip_block(D)] * 4 + [whole((D, D)), whole((VECTORS, D))], after,
        prefetch=1,
        grid=(STRIPS,),
        out_specs=[strip_block(D), strip_block(D), whole((16, 48, D)), whole((8, D))],
        scratch_shapes=[pltpu.VMEM((D, D), F32)],
        out_shape=[pltpu.HBM((STRIPS, SLOTS, D), BF16)] * 2
        + [jax.ShapeDtypeStruct((16, 48, D), BF16), jax.ShapeDtypeStruct((8, D), F32)],
        micros=10,
        mib=22,
        name="middle",
    )


def back_kernel(
    which, at_ref, len_ref, qa_ref, k_ref, v_ref, dctx_ref, ctx_ref, n1_ref,
    grads_ref, d_ref, sums_ref, acc_scr,
):
    d_scr = d_ref.at[0]
    strip = pl.program_id(0)
    lane = lane_iota()
    own = [half_mask(lane, h) for h in (0, 1)]
    length = len_ref[STRIPS * at_ref[0] + strip]
    kx = [key_extra(lane, length, h) for h in (0, 1)]
    vx = [
        jnp.where((lane > 64 * (1 - h)) & (lane < 64 * (1 - h) + 4), 1.0, 0.0).astype(BF16)
        for h in (0, 1)
    ]
    for p in range(GROUP_PAIRS):
        cols = slice(p * 128, p * 128 + 128)
        kp, vp, dp, cp = k_ref[0, :, cols], v_ref[0, :, cols], dctx_ref[0, :, cols], ctx_ref[0, :, cols]
        product = dp.astype(F32) * cp.astype(F32)
        dq, dk, dv = [], [], []
        for h in (0, 1):
            query = qa_ref[0, :, p * 256 + 128 * h : p * 256 + 128 * h + 128]
            inner = jnp.sum(product * own[h].astype(F32), axis=-1, keepdims=True)
            grad = dp * own[h] + pieces_extra(lane, -inner, h, 0.0)
            probs = jnp.exp(dot_bt(kp * own[h] + kx[h], query))
            grad_scores = (probs * dot_bt(vp * own[h] + vx[h], grad)).astype(BF16)
            dv.append(dot(probs.astype(BF16), dp))
            dk.append(dot(grad_scores, query))
            dq.append(dot_at(grad_scores, kp))
        low = lane < 64
        d_scr[:, cols] = (jnp.where(low, dq[0], dq[1]) * (HEAD_DIM**-0.5)).astype(BF16)
        d_scr[:, GCOLS + p * 128 : GCOLS + p * 128 + 128] = jnp.where(low, dk[0], dk[1]).astype(BF16)
        d_scr[:, 2 * GCOLS + p * 128 : 2 * GCOLS + p * 128 + 128] = jnp.where(low, dv[0], dv[1]).astype(BF16)
    d_all = d_scr[...]
    grad = dot_at(n1_ref[0], d_all)
    sums = jnp.sum(d_all.astype(F32), axis=0, keepdims=True)

    @pl.when(strip == 0)
    def _():
        acc_scr[...] = grad
        sums_ref[...] = sums

    @pl.when(strip > 0)
    def _():
        total = (acc_scr[...] + grad).astype(BF16)
        for i in range(16):
            grads_ref[i ^ at_ref[which]] = total[i * 48 : (i + 1) * 48]
        sums_ref[...] += sums


def attend_back(group, which, at, lengths, qa, k, v, dctx, ctx, n1, after):
    def cols(width):
        return pl.BlockSpec((1, SLOTS, width), lambda s, *_: (s, 0, group))

    return call(
        functools.partial(back_kernel, which),
        [at, lengths] + [far(o) for o in (qa, k, v, dctx, ctx, n1)],
        [cols(2 * GCOLS)] + [cols(GCOLS)] * 4 + [strip_block(D)], after,
        prefetch=2,
        grid=(STRIPS,),
        out_specs=[whole((16, 48, D)), strip_block(3 * GCOLS), whole((1, 3 * GCOLS))],
        scratch_shapes=[pltpu.VMEM((D, 3 * GCOLS), F32)],
        out_shape=[jax.ShapeDtypeStruct((16, 48, D), BF16), pltpu.HBM((STRIPS, SLOTS, 3 * GCOLS), BF16),
                   jax.ShapeDtypeStruct((1, 3 * GCOLS), F32)],
        micros=12,
        mib=18,
        name="attend_back",
    )


def end_kernel(
    at_ref, d0_ref, d1_ref, d2_ref, wq_ref, wk_ref, wv_ref, x_ref, gh_ref, vec_ref, mid_ref, s0_ref, s1_ref, s2_ref,
    up0_ref, up1_ref, up2_ref, own_ref, other_ref, small_ref, acc_scr, gp_scr,
):
    strip = pl.program_id(0)
    grad = None
    for g, d_ref in enumerate((d0_ref, d1_ref, d2_ref)):
        for i, w_ref in enumerate((wq_ref, wk_ref, wv_ref)):
            part = dot_bt(d_ref[0, :, i * GCOLS : (i + 1) * GCOLS], w_ref[:, g * GCOLS : (g + 1) * GCOLS])
            grad = part if grad is None else grad + part
    scaled, rstd = norm_parts(x_ref[0].astype(F32))
    t = grad * row_of(vec_ref, GAIN_1)
    cross = jnp.mean(t * scaled, axis=-1, keepdims=True)
    grad_in = rstd * (t - jnp.mean(t, axis=-1, keepdims=True) - scaled * cross)
    gp_scr[...] = (gh_ref[0].astype(F32) + grad_in).astype(BF16)
    core = at_ref[0]
    own_ref[0] = gp_scr[pl.ds(pl.multiple_of(core * HALF, 16), HALF)]
    other_ref[0] = gp_scr[pl.ds(pl.multiple_of((1 - core) * HALF, 16), HALF)]
    sums = [jnp.sum(grad * scaled, axis=0, keepdims=True), jnp.sum(grad, axis=0, keepdims=True)]

    @pl.when(strip == 0)
    def _():
        acc_scr[0:1], acc_scr[1:2] = sums

    @pl.when(strip > 0)
    def _():
        acc_scr[0:1] += sums[0]
        acc_scr[1:2] += sums[1]
        for g, s_ref in enumerate((s0_ref, s1_ref, s2_ref)):
            cols = slice(g * GCOLS, (g + 1) * GCOLS)
            acc_scr[2:3, cols] = s_ref[:, :GCOLS]
            acc_scr[3:4, cols] = s_ref[:, 2 * GCOLS :]
        acc_scr[4:8] = mid_ref[0:4]
        ups = [up0_ref[0], up0_ref[1], up1_ref[0], up2_ref[0]]
        for i, value in enumerate(ups):
            acc_scr[8 + i : 9 + i] = value
        acc_scr[12:16] = jnp.zeros((4, D), F32)
        small_ref[...] = acc_scr[...].astype(BF16)


def end(at, ds, wq, wk, wv, x, gh, vec, mid, sums, ups, after):
    half = pl.BlockSpec((1, HALF, D), lambda s, *_: (s, 0, 0))
    small = [mid, *sums, *ups]
    return call(
        end_kernel, [at, *(far(d) for d in ds), far(wq), far(wk), far(wv), far(x), far(gh), vec, *small],
        [strip_block(D)] * 3 + [whole((D, D))] * 3 + [strip_block(D)] * 2 + [whole((VECTORS, D))]
        + [whole(v.shape) for v in small], after,
        prefetch=1,
        grid=(STRIPS,),
        out_specs=[half, half, whole((SMALL, D))],
        scratch_shapes=[pltpu.VMEM((SMALL, D), F32), pltpu.VMEM((SLOTS, D), BF16)],
        out_shape=[jax.ShapeDtypeStruct((STRIPS, HALF, D), BF16)] * 2 + [jax.ShapeDtypeStruct((SMALL, D), BF16)],
        micros=9,
        mib=24,
        name="end",
    )


def back_in_place_kernel(at_ref, own_ref, got_ref, out_ref):
    mine = (pl.program_id(0) // STRIPS) == at_ref[0]

    @pl.when(mine)
    def _():
        out_ref[...] = own_ref[...]

    @pl.when(jnp.logical_not(mine))
    def _():
        out_ref[...] = got_ref[...]


def back_in_place(at, own, other, after):
    got = swap(other, "seq", 1, 2)
    block = (1, HALF, D)
    spec = pl.BlockSpec(block, lambda i, *_: (lax.rem(i, STRIPS), 0, 0))
    return call(
        back_in_place_kernel, [at, own, got], [spec, spec], after,
        prefetch=1,
        grid=(2 * STRIPS,),
        out_specs=pl.BlockSpec(block, lambda i, *_: (i, 0, 0)),
        out_shape=pltpu.HBM((2 * STRIPS, HALF, D), BF16),
        micros=2,
        mib=8,
        name="in_place",
    )


WIDE = 4


def crossed(i, cross):
    return i // 2 + 2 * lax.rem(i, 2) if cross else i


def widen_mlp_kernel(which, at_ref, mine_ref, other_ref, *rest):
    down_ref, up_ref = rest[-2:]
    swapped = at_ref[0] == 1
    place = lax.rem(at_ref[which], WIDE)
    for i in range(WIDE):
        mine, other = mine_ref[i ^ place], other_ref[i ^ place]
        down_ref[i * 96 : i * 96 + 96] = jnp.where(swapped, other, mine).astype(F32)
        up = jnp.where(swapped, mine, other).astype(F32)
        up_ref[i * 48 : i * 48 + 48, :D] = up[:48]
        up_ref[i * 48 : i * 48 + 48, D:] = up[48:]


def widen_mlp(part, at, p, given, after):
    which = p.which
    block = pl.BlockSpec(
        (WIDE, FCALL // 16, D), lambda i, at_ref: (crossed(i, p.cross) ^ (at_ref[which] // WIDE), 0, 0)
    )
    given = [far(v) for v in given]
    return call(
        functools.partial(widen_mlp_kernel, which), [at, p.total, p.got] + given,
        [block, block] + [pl.BlockSpec(memory_space=pl.ANY)] * len(given), after,
        prefetch=1,
        grid=(16 // WIDE,),
        out_specs=[
            pl.BlockSpec((WIDE * FCALL // 16, D), lambda i, *_: (16 // WIDE * part + i, 0)),
            pl.BlockSpec((WIDE * D // 16, FCALL), lambda i, *_: (i, part)),
        ],
        out_shape=[pltpu.HBM((FF, D), F32), pltpu.HBM((D, FF), F32)],
        input_output_aliases={3: 0, 4: 1} if given else {},
        micros=4,
        mib=12,
        name="widen_mlp",
    )


def widen_attn_kernel(w0, w1, cross1, at_ref, m0_ref, o0_ref, m1_ref, o1_ref, out_ref, q_ref, k_ref, v_ref, small_ref):
    swapped = at_ref[0] == 1
    first, second = lax.rem(at_ref[w0], WIDE), lax.rem(at_ref[w1], WIDE)
    block1 = crossed(pl.program_id(0), cross1) ^ (at_ref[w1] // WIDE)
    for i in range(WIDE):
        rows = slice(i * 48, i * 48 + 48)
        m0, o0 = m0_ref[i ^ first].astype(F32), o0_ref[i ^ first].astype(F32)
        at1 = pl.ds(pl.multiple_of((block1 * WIDE + (i ^ second)) * 48, 16), 48)
        m1, o1 = m1_ref[at1].astype(F32), o1_ref[at1].astype(F32)
        out_ref[rows] = jnp.where(swapped, o0, m0)
        blocks = (jnp.where(swapped, m0, o0), jnp.where(swapped, o1, m1), jnp.where(swapped, m1, o1))
        for g, block in enumerate(blocks):
            cols = slice(g * GCOLS, (g + 1) * GCOLS)
            q_ref[rows, cols] = block[:, :GCOLS]
            k_ref[rows, cols] = block[:, GCOLS : 2 * GCOLS]
            v_ref[rows, cols] = block[:, 2 * GCOLS :]
    small_ref[...] = m1_ref[16 * 48 :].astype(F32) + o1_ref[16 * 48 :].astype(F32)


def widen_attn(at, p0, p1, after):
    w0, w1 = p0.which, p1.which
    block = pl.BlockSpec((WIDE, 48, D), lambda i, at_ref: (crossed(i, p0.cross) ^ (at_ref[w0] // WIDE), 0, 0))
    rows = whole((16 * 48 + SMALL, D))
    return call(
        functools.partial(widen_attn_kernel, w0, w1, p1.cross), [at, p0.total, p0.got, p1.total, p1.got], [block, block, rows, rows], after,
        prefetch=1,
        grid=(16 // WIDE,),
        out_specs=[pl.BlockSpec((WIDE * 48, D), lambda i, *_: (i, 0))] * 4 + [whole((SMALL, D))],
        out_shape=[jax.ShapeDtypeStruct((D, D), F32)] * 4 + [jax.ShapeDtypeStruct((SMALL, D), F32)],
        micros=4,
        mib=16,
        name="widen_attn",
    )


def swap(value, axis, bit, size):
    return lax.ppermute(value, axis, [(i, i ^ bit) for i in range(size)])


TAIL = (
    "b", "a", "b", "0", "1", "a", "b", "0", "a", "1", "end", "b", "1", "a",
    "b", "place", "0", "b", "a", "1", "wide", "b", "out", "a", "b", "1",
)


class Sum:
    def __init__(self, order, back, dp, keep=None, send=None, pick=None):
        self.keep, self.send, self.pick, self.small = keep, send, pick, None
        rest = [1 << i for i in range(4, dp.bit_length() - 1)]
        hops = [("seq", 1, 2, "half"), ("dp", order[:2], dp, "quad")] + [("dp", b, dp, "half") for b in order[2:]]
        hops += [("dp", b, dp, "whole") for b in rest]
        hops += [("dp", b, dp, "join") for b in back] + [("seq", 1, 2, "pair")]
        self.hops, self.total, self.got = hops, None, None
        self.which = 1 if back[-1] == 1 else 2
        self.cross = back[-1] != order[0]

    def start(self):
        axis, bit, size, kind = self.hops[0]
        if kind == "quad":
            masks = (bit[1], bit[0], bit[0] | bit[1])
            self.got = [swap(part, axis, mask, size) for part, mask in zip(self.send, masks)]
            return
        self.got = swap(self.send if kind == "half" else self.total, axis, bit, size)


TAKES = {"load": 3, "quad": 4}
GIVES = {"pick": 2, "split": 2, "quad": 2, "split4": 4}


def merge_kernel(kinds, *refs):
    at_ref, refs = refs[0], refs[1:]
    outs = refs[sum(TAKES.get(kind, 2) for kind in kinds) :]
    for kind in kinds:
        (a, b, *more), refs = refs[: TAKES.get(kind, 2)], refs[TAKES.get(kind, 2) :]
        if kind == "pick":
            keep, send = outs[:2]

            @pl.when(at_ref[0] == 0)
            def _():
                keep[...], send[...] = a[...], b[...]

            @pl.when(at_ref[0] != 0)
            def _():
                keep[...], send[...] = b[...], a[...]

        elif kind == "split":
            half = a.shape[0] // 2
            outs[0][...] = a[:half] + b[:half]
            outs[1][...] = a[half:] + b[half:]
        elif kind == "add":
            outs[0][...] = a[...] + b[...]
        elif kind == "load":
            rows = a.shape[1]
            outs[0][:rows] = a[0] + b[0]
            outs[0][rows:] = more[0][...]
        elif kind == "split4":
            part = a.shape[0] // 4
            for i in range(4):
                outs[i][...] = a[i * part : (i + 1) * part] + b[i * part : (i + 1) * part]
        elif kind == "quad":
            half = a.shape[0] // 2
            for i in range(2):
                rows = slice(i * half, (i + 1) * half)
                total = a[rows].astype(F32) + b[rows].astype(F32)
                outs[i][...] = (total + (more[0][rows].astype(F32) + more[1][rows].astype(F32))).astype(BF16)
        elif kind == "join":
            half = a.shape[0]
            outs[0][:half] = a[...]
            outs[0][half:] = b[...]
        else:
            rows = a.shape[0] - SMALL
            outs[0][:rows], outs[0][rows : 2 * rows] = a[:rows], b[:rows]
            outs[0][2 * rows :] = a[rows:] + b[rows:]
        outs = outs[GIVES.get(kind, 1) :]


def merge(at, pieces, after):
    kinds, operands, shapes = [], [], []
    for p in pieces:
        if p.pick:
            kind, args = "pick", list(p.pick)
        else:
            kind = p.hops.pop(0)[3]
            args = [p.keep, *p.got] if kind == "quad" else [p.keep if kind == "half" else p.total, p.got]
            if kind == "half":
                kind = {"half": "split", "quad": "split4"}.get(p.hops[0][3], "add")
            elif kind == "whole":
                kind = "add"
            if p.small is not None and kind == "add" and p.hops[0][3] == "join":
                kind, args = "load", args + [p.small]
            elif p.small is not None and kind == "join":
                kind = "carry"
        n, tail = args[0].shape[0], args[0].shape[1:]
        n = {"pick": [n, n], "split": [n // 2, n // 2], "add": [n], "join": [2 * n], "carry": [2 * n - SMALL],
             "load": [1], "split4": [n // 4] * 4, "quad": [n // 2] * 2}[kind]
        kinds.append(kind)
        operands += args
        shapes.append([(tail[0] + SMALL, D)] if kind == "load" else [(m,) + tail for m in n])
    flat = [shape for group in shapes for shape in group]
    outs = list(call(
        functools.partial(merge_kernel, kinds),
        [at] + [pltpu.with_memory_space_constraint(v, pltpu.VMEM) for v in operands],
        [pl.BlockSpec(memory_space=pltpu.VMEM)] * len(operands), after,
        prefetch=1,
        grid=(1,),
        out_specs=[pl.BlockSpec(memory_space=pltpu.VMEM)] * len(flat),
        out_shape=[pltpu.VMEM(shape, BF16) for shape in flat],
        micros=2,
        mib=6,
        name="merge",
    ))
    made = list(outs)
    for p, kind in zip(pieces, kinds):
        p.pick = None
        if kind == "split4":
            p.keep, p.send, outs = outs[0], outs[1:4], outs[4:]
        elif kind in ("pick", "split", "quad"):
            p.keep, p.send, outs = outs[0], outs[1], outs[2:]
        else:
            p.total, outs = outs[0], outs[1:]
        p.start()
    return made


def local(
    dp, patches, lengths, gain_one, shift_one, w_query, b_query, w_key, w_value, b_value, w_out, b_out,
    gain_two, shift_two, w_up, b_up, w_down, b_down, cotangent,
):
    core, block = lax.axis_index("seq"), lax.axis_index("dp")
    x_first, y_first = (1, 2, 4, 8), (2, 1, 4, 8)

    def place_of(order):
        return sum(jnp.where((block & bit) != 0, 8 >> i, 0) for i, bit in enumerate(order))

    at = jnp.stack([core, place_of(x_first), place_of(y_first)]).astype(jnp.int32)
    foreign = lambda v: lax.dynamic_slice(v, (STRIPS * (1 - core), 0, 0), (STRIPS, HALF, D))
    got = swap(foreign(patches), "seq", 1, 2)
    got_cot = swap(foreign(cotangent), "seq", 1, 2)
    vectors = (gain_one, shift_one, b_query, b_value, b_out, gain_two, shift_two, b_down, b_up)
    vec = jnp.concatenate(vectors).reshape(VECTORS, D)
    n1, qa, k, v, ctx, hid, n2, x, cot = attend(
        at, lengths, patches, got, cotangent, got_cot, vec, w_query, w_key, w_value, w_out
    )
    flat = lambda v: v.reshape(ROWS, D)
    shared = (at, flat(n2), flat(cot), w_up, w_down, vec)
    keep, send, gn, up_0, acc = mlp(0, 2, 1, *shared, flat(hid), None, None, [])
    m0 = Sum(x_first, Y_LAST, dp, keep, send)
    m0.start()
    keep, send, gn, up_1, acc = mlp(2, 1, 1, *shared, acc, gn, None, [])
    made = merge(at, [m0], [gn])
    keep, send, gn, up_2, _, out_own, out_other = mlp(3, 1, 1, *shared, acc, gn, (keep, send), made)
    m1 = Sum(x_first, Y_LAST, dp, keep, send)
    m1.start()
    gh, dctx, g_out, sums_mid = middle(1, at, gn.reshape(STRIPS, SLOTS, D), hid, cot, ctx, w_out, vec, [send])
    made = merge(at, [m0, m1], [g_out])
    back = (at, lengths, qa, k, v, dctx, ctx, n1)
    grads_0, d_0, sums_0 = attend_back(0, 1, *back, made)
    a0 = Sum(x_first, X_LAST, dp, pick=(g_out, grads_0))
    made = merge(at, [m0, a0], [grads_0])
    grads_1, d_1, sums_1 = attend_back(1, 1, *back, made)
    made = merge(at, [m0, m1, a0], [grads_1])
    grads_2, d_2, sums_2 = attend_back(2, 1, *back, made)
    a1 = Sum(x_first, X_LAST, dp, pick=(grads_1, grads_2))
    made = merge(at, [m0, m1, a0, a1], [grads_2])
    pieces = {"0": m0, "1": m1, "a": a0, "b": a1}
    for turn in TAIL:
        if turn == "end":
            gp_own, gp_other, a1.small = end(
                at, (d_0, d_1, d_2), w_query, w_key, w_value, x, gh, vec, sums_mid, (sums_0, sums_1, sums_2),
                (up_0, up_1, up_2), made,
            )
            for bit in range(4, dp.bit_length() - 1):
                a1.small = a1.small + swap(a1.small, "dp", 1 << bit, dp)
            made = [a1.small]
        elif turn == "place":
            grad_patches = back_in_place(at, gp_own, gp_other, made)
            made = [far(grad_patches)]
        elif turn == "out":
            output = back_in_place(at, out_own, out_other, made)
            made = [far(output)]
        elif turn == "wide":
            given = widen_mlp(0, at, m0, (), made)
            made = [far(given[0])]
        else:
            made = merge(at, [pieces[c] for c in turn], made)
    for p in pieces.values():
        while len(p.hops) > 1:
            made = merge(at, [p], made)
    g_out, g_query, g_key, g_value, small = widen_attn(at, a0, a1, [])
    g_down, g_up = widen_mlp(1, at, m1, given, [])
    small = small.reshape(-1)
    vecs = [small[i * D : (i + 1) * D] for i in range(8)]
    g_bup = small[8 * D : 8 * D + FF]
    return (
        output, grad_patches, vecs[0], vecs[1], g_query, vecs[2], g_key, g_value, vecs[3], g_out, vecs[6],
        vecs[4], vecs[5], g_up, g_bup, g_down, vecs[7],
    )


def solution(mesh):
    dp = mesh.shape["dp"]
    rows, rep = P("dp", "seq", None), P()
    return jax.shard_map(
        functools.partial(local, dp),
        mesh=mesh,
        in_specs=(rows, P("dp")) + (rep,) * 15 + (rows,),
        out_specs=(rows, rows) + (rep,) * 15,
        check_vma=False,
    )
```
